256 devices in a mesh: outer: 4 (over x), member: 64 (over y, z, core).
Axes of the slice: x: 4, y: 4, z: 8, core: 2. Of those that a mesh axis runs over, the one named last changes fastest.
Arguments:
- embeds: bfloat16 [524288, 768], P(('outer', 'member')), parts along dimension 0, as said below
- cluster_id: int32 [524288], P(('outer', 'member')), parts along dimension 0, may hold values from 0 to 255, as said below
- row_index: int32 [524288], P(('outer', 'member')), parts along dimension 0, may hold values from 0 to 131071, each once
Outputs:
- nearest: float32 [524288], P(('outer', 'member')), parts along dimension 0
The draws below stay inside these ranges and needn't reach their ends.
There are 4 independent parts, one for each index of `outer`. The reference program is written for one: setup_inputs(seed, part) draws one part's arguments, and reference() takes and returns one part's arrays. A program takes and returns all parts, laid end to end along the dimension named above; each array names one. Nothing has to cross between parts.
Inputs may be any that keep to these rules, and one draw needn't show every extreme that they name: `cluster_id`: no cluster has more than 16 rows on one device; one cluster has exactly 16 rows on every device; the clusters of each owner hold exactly 256 / (devices of member) * 8 rows of every device. `embeds`: Real-valued rows with no zero row.
All inputs are finite; a program needn't handle non-finite values.
Results may differ from the reference program's by a relative error of at most 0.00063.
Values may be sent and summed in bfloat16 or wider, within the bound.
No kernel may reach another device: no remote copies, remote signals or barrier semaphores. Data moves between devices by JAX's collectives and lax.ppermute only.
A program may use at most 64 MiB of HBM per device.

```python
import jax
import jax.numpy as jnp
from jax import lax

D = 768
CLUSTERS = 256
ROWS_DEV = 2048
MOST = 16
ROWS = 131072


def common_layout(key):
    key = jax.random.fold_in(key, 11)
    key_size, key_side, key_force, key_order = jax.random.split(key, 4)
    half = MOST // 2
    devices = ROWS // ROWS_DEV
    pairs = CLUSTERS // 2
    size = jax.random.randint(key_size, (devices, pairs), 0, half + 1)
    side = jax.random.randint(key_side, (devices, pairs), 0, 2)
    forced = jax.random.randint(key_force, (), 0, CLUSTERS)
    pair_ids = jnp.arange(pairs, dtype=jnp.int32)
    size = jnp.where(pair_ids[None, :] == forced // 2, half, size)
    side = jnp.where(pair_ids[None, :] == forced // 2, forced % 2, side)
    even = half + size * (1 - 2 * side)
    odd = MOST - even
    counts = jnp.stack([even, odd], axis=2).reshape(devices, CLUSTERS)
    slot_ids = jnp.arange(CLUSTERS, dtype=jnp.int32)
    listed = jax.vmap(lambda c: jnp.repeat(slot_ids, c, total_repeat_length=ROWS_DEV))(counts)
    keys = jax.random.split(key_order, devices)
    shuffled = jax.vmap(lambda k, row: jax.random.permutation(k, row))(keys, listed)
    return shuffled.reshape(ROWS).astype(jnp.int32)


def draw_cluster_id(key, part):
    return common_layout(key)


def draw_embeds(key, part):
    clusters = common_layout(key)
    key = jax.random.fold_in(key, 5)
    key_fam, key_base, key_noise, key_spread = jax.random.split(key, 4)
    devices = ROWS // ROWS_DEV
    families = max(1, devices * MOST // 8)
    family = clusters * families + jax.random.randint(key_fam, (ROWS,), 0, families)
    base = jax.vmap(lambda f: jax.random.normal(jax.random.fold_in(key_base, f), (D,), jnp.float32))(family)
    spread = jnp.exp(jax.random.uniform(key_spread, (ROWS, 1), jnp.float32, jnp.log(0.3), jnp.log(3.0)))
    noise = jax.random.normal(key_noise, (ROWS, D), jnp.float32)
    return ((base + spread * noise) * 0.5).astype(jnp.bfloat16)


def setup_inputs(seed: int = 0, part: int = 0) -> dict:
    key_list = jax.random.split(jax.random.key(seed), 4)
    part_splits = jax.random.split(jax.random.fold_in(key_list[3], part), 4)
    return {
        "embeds": draw_embeds(jax.random.fold_in(jax.random.fold_in(key_list[3], part), 71), part),
        "cluster_id": draw_cluster_id(jax.random.fold_in(jax.random.fold_in(key_list[3], part), 71), part),
        "row_index": jax.random.permutation(part_splits[2], ROWS).astype(jnp.int32),
    }


def reference(embeds, cluster_id, row_index):
    whole = embeds.astype(jnp.float32)
    inverse = lax.rsqrt(lax.optimization_barrier(jnp.sum(whole * whole, axis=1, keepdims=True)) + 1e-06)
    unit = (whole * inverse).astype(jnp.bfloat16)
    unit_wide = unit.astype(jnp.float32)
    devices = ROWS // ROWS_DEV
    labels = jnp.arange(CLUSTERS, dtype=jnp.int32)

    def ranks(block):
        match = (block[:, None] == labels[None, :]).astype(jnp.int32)
        return lax.optimization_barrier(jnp.sum((jnp.cumsum(match, axis=0) - 1) * match, axis=1))
    rank = lax.map(ranks, cluster_id.reshape(devices, ROWS_DEV)).reshape(ROWS)
    position = jnp.arange(ROWS, dtype=jnp.int32)
    column = position // ROWS_DEV * MOST + rank
    table = jnp.full((CLUSTERS, devices * MOST), -1, jnp.int32).at[cluster_id, column].set(position)

    def one(members):
        valid = members >= 0
        safe = jnp.where(valid, members, 0)
        rows = unit_wide[safe]
        order = jnp.where(valid, row_index[safe], -1)
        scores = jnp.dot(rows, rows.T, precision=lax.Precision.HIGHEST)
        keep = (order[None, :] < order[:, None]) & (order[None, :] >= 0)
        return jnp.maximum(lax.optimization_barrier(jnp.max(jnp.where(keep, scores, -1.0), axis=1)), -1.0)
    best = lax.map(one, table)
    target = jnp.where(table >= 0, table, ROWS)
    nearest = jnp.full((ROWS,), -1.0, jnp.float32).at[target.reshape(-1)].set(best.reshape(-1).astype(jnp.float32), mode='drop')
    return nearest
```

```python
import functools

import jax
import jax.numpy as jnp
from jax import lax
from jax.experimental import pallas as pl
from jax.experimental.pallas import tpu as pltpu
from jax.sharding import PartitionSpec as P

CLUSTERS = 256
INDEX_BITS = 17
LANES = 128
META = 8


def iota(shape, dim):
    return lax.broadcasted_iota(jnp.int32, shape, dim)


def wide_row(ref):
    return jnp.concatenate([ref[b : b + 1, :] for b in range(ref.shape[0])], axis=1)


def send_kernel(owners, per_owner, per_pair, cid_ref, idx_ref, emb_ref, out_ref, pos_ref, pos_scr, meta_scr):
    rows, width = emb_ref.shape
    step = pl.program_id(0)
    per_step = out_ref.shape[0]
    size = per_step * per_pair

    @pl.when(step == 0)
    def _():
        cid = wide_row(cid_ref)
        idx = wide_row(idx_ref)
        owner = cid // per_owner
        hit = iota((owners, rows), 0) == owner
        hot = hit.astype(jnp.bfloat16)
        tile = 256
        before = (iota((tile, tile), 0) < iota((tile, tile), 1)).astype(jnp.bfloat16)
        carry = jnp.zeros((owners, 1), jnp.float32)
        ranks = []
        for b in range(rows // tile):
            part = hot[:, b * tile : (b + 1) * tile]
            wide = part.astype(jnp.float32)
            count = jnp.dot(part, before, preferred_element_type=jnp.float32) + carry
            ranks.append(jnp.sum(count * wide, axis=0, keepdims=True))
            carry = carry + jnp.sum(wide, axis=1, keepdims=True)
        rank = jnp.concatenate(ranks, axis=1).astype(jnp.int32)
        pos = owner * per_pair + rank
        pos_scr[...] = pos
        for b in range(pos_ref.shape[0]):
            pos_ref[b : b + 1, :] = pos[:, b * LANES : (b + 1) * LANES]
        key = (cid - owner * per_owner) * (1 << INDEX_BITS) + idx
        slot = iota((per_pair, rows), 0) == rank
        pieces = (key & 255, (key >> 8) & 255, key >> 16)
        spread = [jnp.where(slot, p.astype(jnp.float32), 0.0).astype(jnp.bfloat16) for p in pieces]
        spread.append(jnp.zeros((LANES - 3 * per_pair, rows), jnp.bfloat16))
        spread = jnp.concatenate(spread, axis=0)
        meta_scr[...] = lax.dot_general(
            hot, spread, (((1,), (1,)), ((), ())), preferred_element_type=jnp.float32
        )

    pick = (iota((size, rows), 0) + step * size == pos_scr[...]).astype(jnp.bfloat16)
    moved = jnp.dot(pick, emb_ref[...], preferred_element_type=jnp.float32)
    inverse = lax.rsqrt(jnp.sum(moved * moved, axis=1, keepdims=True) + 1e-06)
    unit = (moved * inverse).astype(jnp.bfloat16)
    for c in range(width // LANES):
        out_ref[:, c * per_pair : (c + 1) * per_pair, :] = unit[:, c * LANES : (c + 1) * LANES].reshape(
            per_step, per_pair, LANES
        )
    meta = meta_scr[pl.ds(pl.multiple_of(step * per_step, per_step), per_step), :]
    meta = jnp.broadcast_to(meta[:, None, :], (per_step, META, LANES)).astype(jnp.bfloat16)
    out_ref[:, (width // LANES) * per_pair :, :] = meta


def best_kernel(per_pair, got_ref, out_ref, x_scr, col_scr, row_scr):
    senders = got_ref.shape[0]
    rows, width = x_scr.shape
    step = pl.program_id(0)
    size = 256

    @pl.when(step == 0)
    def _():
        for c in range(width // LANES):
            x_scr[:, c * LANES : (c + 1) * LANES] = got_ref[:, c * per_pair : (c + 1) * per_pair, :].reshape(
                rows, LANES
            )
        meta = got_ref[:, (width // LANES) * per_pair :, :].astype(jnp.float32)[:, 0:1, :]
        meta = jnp.broadcast_to(meta, (senders, per_pair, LANES)).reshape(rows, LANES)
        own = (iota((rows, LANES), 0) % per_pair) == (iota((rows, LANES), 1) % per_pair)
        meta = jnp.where(own, meta, 0.0).astype(jnp.bfloat16)

        def weights(lane):
            piece = lane // per_pair
            value = jnp.where(piece == 0, 1.0, jnp.where(piece == 1, 256.0, jnp.where(piece == 2, 65536.0, 0.0)))
            return value.astype(jnp.bfloat16)

        col_scr[...] = jnp.dot(meta, weights(iota((LANES, LANES), 0)), preferred_element_type=jnp.float32)
        row_scr[...] = lax.dot_general(
            weights(iota((8, LANES), 1)), meta, (((1,), (1,)), ((), ())), preferred_element_type=jnp.float32
        )

    start = pl.multiple_of(step * size, size)
    mine = x_scr[pl.ds(start, size), :]
    key = row_scr[0:1, pl.ds(start, size)]
    span = float(1 << INDEX_BITS)
    base = jnp.floor(key * (1.0 / span)) * span
    best = jnp.full((1, size), -1.0, jnp.float32)
    chunk = 512
    for j in range(rows // chunk):
        other = x_scr[j * chunk : (j + 1) * chunk, :]
        scores = lax.dot_general(other, mine, (((1,), (1,)), ((), ())), preferred_element_type=jnp.float32)
        col = col_scr[j * chunk : (j + 1) * chunk, :]
        col = jnp.concatenate([col] * (size // LANES), axis=1)
        keep = (col < key) & (col >= base)
        best = jnp.maximum(best, jnp.max(jnp.where(keep, scores, -1.0), axis=0, keepdims=True))
    for b in range(size // LANES):
        out_ref[pl.ds(step * (size // LANES) + b, 1), :] = best[:, b * LANES : (b + 1) * LANES]


def home_kernel(ret_ref, pos_ref, out_ref):
    owners, per_pair = ret_ref.shape
    pos = wide_row(pos_ref)
    rows = pos.shape[1]
    owner = pos // per_pair
    rank = pos - owner * per_pair
    slot = (iota((per_pair, rows), 0) == rank).astype(jnp.bfloat16)
    rest = ret_ref[...]
    spread = jnp.zeros((owners, rows), jnp.float32)
    for _ in range(3):
        part = rest.astype(jnp.bfloat16)
        rest = rest - part.astype(jnp.float32)
        spread = spread + jnp.dot(part, slot, preferred_element_type=jnp.float32)
    mine = jnp.where(iota((owners, rows), 0) == owner, spread, 0.0)
    nearest = jnp.sum(mine, axis=0, keepdims=True)
    for b in range(out_ref.shape[0]):
        out_ref[b : b + 1, :] = nearest[:, b * LANES : (b + 1) * LANES]


def whole(shape):
    return pl.BlockSpec(shape, lambda *_: (0,) * len(shape))


LIMIT = pltpu.CompilerParams(vmem_limit_bytes=48 * 1024 * 1024)


def on_device(embeds, cluster_id, row_index):
    members = lax.axis_size("member")
    rows, width = embeds.shape
    per_owner = CLUSTERS // members
    per_pair = rows // members
    lines = rows // LANES
    tall = width // LANES * per_pair + META
    steps = 4
    payload, pos = pl.pallas_call(
        functools.partial(send_kernel, members, per_owner, per_pair),
        grid=(steps,),
        in_specs=[whole((lines, LANES)), whole((lines, LANES)), whole((rows, width))],
        out_specs=[
            pl.BlockSpec((members // steps, tall, LANES), lambda s: (s, 0, 0)),
            whole((lines, LANES)),
        ],
        out_shape=[
            jax.ShapeDtypeStruct((members, tall, LANES), jnp.bfloat16),
            jax.ShapeDtypeStruct((lines, LANES), jnp.int32),
        ],
        scratch_shapes=[
            pltpu.VMEM((1, rows), jnp.int32),
            pltpu.VMEM((members, LANES), jnp.float32),
        ],
        compiler_params=LIMIT,
        name="send",
    )(cluster_id.reshape(lines, LANES), row_index.reshape(lines, LANES), embeds)
    got = lax.all_to_all(payload, "member", split_axis=0, concat_axis=0, tiled=True)
    best = pl.pallas_call(
        functools.partial(best_kernel, per_pair),
        grid=(rows // 256,),
        in_specs=[whole((members, tall, LANES))],
        out_specs=whole((lines, LANES)),
        out_shape=jax.ShapeDtypeStruct((lines, LANES), jnp.float32),
        scratch_shapes=[
            pltpu.VMEM((rows, width), jnp.bfloat16),
            pltpu.VMEM((rows, LANES), jnp.float32),
            pltpu.VMEM((8, rows), jnp.float32),
        ],
        compiler_params=LIMIT,
        name="best",
    )(got)
    back = lax.all_to_all(best.reshape(members, per_pair), "member", split_axis=0, concat_axis=0, tiled=True)
    nearest = pl.pallas_call(
        home_kernel,
        out_shape=jax.ShapeDtypeStruct((lines, LANES), jnp.float32),
        compiler_params=LIMIT,
        name="home",
    )(back, pos)
    return nearest.reshape(rows)


def solution(mesh):
    in_specs = (P(("outer", "member"), None), P(("outer", "member")), P(("outer", "member")))
    out_specs = P(("outer", "member"))
    return jax.shard_map(
        on_device, mesh=mesh, in_specs=in_specs, out_specs=out_specs, check_vma=False
    )
```

```python
import functools

import jax
import jax.numpy as jnp
from jax import lax
from jax.experimental import pallas as pl
from jax.experimental.pallas import tpu as pltpu
from jax.sharding import PartitionSpec as P

CLUSTERS = 256
INDEX_BITS = 17
LANES = 128
META = 8
TILE = 256
NZ, CORES, PLANE = 8, 2, 8
EARLY = (4, 3, 5, 0)
LATE = (2, 6, 1, 7)
ORDER = EARLY + LATE
BF16, F32, I32 = jnp.bfloat16, jnp.float32, jnp.int32


def iota(shape, dim):
    return lax.broadcasted_iota(I32, shape, dim)


def dot(a, b):
    return jnp.dot(a, b, preferred_element_type=F32)


def dot_t(a, b):
    return lax.dot_general(a, b, (((1,), (1,)), ((), ())), preferred_element_type=F32)


def wide_row(ref):
    return jnp.concatenate([ref[b : b + 1, :] for b in range(ref.shape[0])], axis=1)


def put_row(ref, row):
    for b in range(ref.shape[0]):
        ref[b : b + 1, :] = row[:, b * LANES : (b + 1) * LANES]


def my_z():
    return (lax.axis_index("member") // CORES) % NZ


def shift_plane(owner):
    dz = ((owner // CORES) % NZ + NZ - my_z()) % NZ
    return dz, owner // (CORES * NZ) * CORES + owner % CORES


def route(owners, per_owner, per_pair, cid, idx):
    rows = cid.shape[1]
    owner = cid // per_owner
    dz, plane = shift_plane(owner)
    hot = (iota((owners, rows), 0) == dz * PLANE + plane).astype(BF16)
    before = (iota((TILE, TILE), 0) < iota((TILE, TILE), 1)).astype(BF16)
    carry = jnp.zeros((owners, 1), F32)
    ranks = []
    for b in range(rows // TILE):
        part = hot[:, b * TILE : (b + 1) * TILE]
        wide = part.astype(F32)
        ranks.append(jnp.sum((dot(part, before) + carry) * wide, axis=0, keepdims=True))
        carry = carry + jnp.sum(wide, axis=1, keepdims=True)
    rank = jnp.concatenate(ranks, axis=1).astype(I32)
    key = (cid - owner * per_owner) * (1 << INDEX_BITS) + idx
    slot = iota((per_pair, rows), 0) == rank
    pieces = (key & 255, (key >> 8) & 255, key >> 16)
    spread = [jnp.where(slot, p.astype(F32), 0.0).astype(BF16) for p in pieces]
    spread.append(jnp.zeros((LANES - 3 * per_pair, rows), BF16))
    meta = dot_t(hot, jnp.concatenate(spread, axis=0))
    return owner * per_pair + rank, meta


def place(pos, per_pair, shifts, inner):
    owner = pos // per_pair
    rank = pos - owner * per_pair
    dz, plane = shift_plane(owner)
    goal = jnp.full(pos.shape, -1, I32)
    for k, shift in enumerate(shifts):
        slot = plane * len(shifts) + k if inner else k * PLANE + plane
        goal = jnp.where(dz == shift, slot * per_pair + rank, goal)
    return goal


def unit_rows(goal, first, size, emb):
    pick = (iota((size, emb.shape[0]), 0) + first == goal).astype(BF16)
    moved = dot(pick, emb)
    inverse = lax.rsqrt(jnp.sum(moved * moved, axis=1, keepdims=True) + 1e-06)
    return (moved * inverse).astype(BF16)


def pack(unit, meta, per_pair):
    blocks = unit.shape[0] // per_pair
    parts = [
        unit[:, c * LANES : (c + 1) * LANES].reshape(blocks, per_pair, LANES)
        for c in range(unit.shape[1] // LANES)
    ]
    parts.append(jnp.broadcast_to(meta[:, None, :], (blocks, META, LANES)).astype(BF16))
    return parts


def put_parts(ref, parts):
    at = 0
    for part in parts:
        ref[..., at : at + part.shape[-2], :] = part
        at += part.shape[-2]


def first_kernel(
    owners, per_owner, per_pair, cid_hbm, idx_hbm, emb_hbm, out_ref, pos_ref, meta_ref, flag_ref,
    cid_ref, idx_ref, emb_ref, sem
):
    copies = [
        pltpu.make_async_copy(src, dst, sem.at[n])
        for n, (src, dst) in enumerate(((cid_hbm, cid_ref), (idx_hbm, idx_ref), (emb_hbm, emb_ref)))
    ]
    for copy in copies:
        copy.start()
    copies[0].wait()
    copies[1].wait()
    pos, meta = route(owners, per_owner, per_pair, wide_row(cid_ref), wide_row(idx_ref))
    put_row(pos_ref, pos)
    meta_ref[...] = meta
    flag_ref[0] = 1
    copies[2].wait()
    unit = unit_rows(place(pos, per_pair, EARLY[:1], False), 0, PLANE * per_pair, emb_ref[...])
    shift = EARLY[0]
    put_parts(out_ref, pack(unit, meta[shift * PLANE : (shift + 1) * PLANE], per_pair))


def some_kernel(per_pair, shifts, pos_ref, meta_ref, emb_hbm, *refs):
    *outs, emb_ref, sem = refs
    copy = pltpu.make_async_copy(emb_hbm, emb_ref, sem)
    copy.start()
    goal = place(wide_row(pos_ref), per_pair, shifts, False)
    copy.wait()
    size = PLANE * per_pair
    unit = unit_rows(goal, 0, size * len(outs), emb_ref[...])
    for k, (shift, out_ref) in enumerate(zip(shifts, outs)):
        meta = meta_ref[shift * PLANE : (shift + 1) * PLANE, :]
        put_parts(out_ref, pack(unit[k * size : (k + 1) * size], meta, per_pair))


def late_kernel(per_pair, pos_ref, meta_ref, emb_hbm, out_ref, emb_ref, goal_scr, sem):
    step = pl.program_id(0)
    per_step = out_ref.shape[0]
    size = per_step * len(LATE) * per_pair

    @pl.when(step == 0)
    def _():
        copy = pltpu.make_async_copy(emb_hbm, emb_ref, sem)
        copy.start()
        goal_scr[...] = place(wide_row(pos_ref), per_pair, LATE, True)
        copy.wait()

    unit = unit_rows(goal_scr[...], step * size, size, emb_ref[...])
    for p in range(per_step):
        for k, shift in enumerate(LATE):
            at = (p * len(LATE) + k) * per_pair
            meta = meta_ref[pl.ds(shift * PLANE + step * per_step + p, 1), :]
            parts = pack(unit[at : at + per_pair], meta, per_pair)
            put_parts(out_ref.at[p, k], [part[0] for part in parts])


def piece_weights(lane, per_pair):
    piece = lane // per_pair
    value = jnp.where(piece == 0, 1.0, jnp.where(piece == 1, 256.0, jnp.where(piece == 2, 65536.0, 0.0)))
    return value.astype(BF16)


def best_kernel(per_pair, early_ref, *refs):
    *late, out_ref, col_scr, base_scr, row_scr, across_scr = refs
    rows = col_scr.shape[0]
    blocks = [early_ref.at[:, k] for k in range(len(EARLY))] + list(late)
    chunks = early_ref.shape[2] // per_pair
    span = float(1 << INDEX_BITS)

    def tile(t):
        return jnp.concatenate(
            [blocks[t][:, c * per_pair : (c + 1) * per_pair, :].reshape(TILE, LANES) for c in range(chunks)], axis=1
        )

    meta = [block[:, chunks * per_pair :, :].astype(F32)[:, 0:1, :] for block in blocks]
    meta = jnp.concatenate(meta, axis=0)
    meta = jnp.broadcast_to(meta, (rows // per_pair, per_pair, LANES)).reshape(rows, LANES)
    own = (iota((rows, LANES), 0) % per_pair) == (iota((rows, LANES), 1) % per_pair)
    meta = jnp.where(own, meta, 0.0).astype(BF16)
    col = dot(meta, piece_weights(iota((LANES, LANES), 0), per_pair))
    col_scr[...] = col
    base_scr[...] = jnp.floor(col * (1.0 / span)) * span
    row_scr[...] = dot_t(piece_weights(iota((8, LANES), 1), per_pair), meta)
    across_scr[...] = jnp.full(across_scr.shape, -1.0, F32)

    down = []
    for i in range(rows // TILE):
        mine = tile(i)
        row = [row_scr[0:1, i * TILE + b : i * TILE + b + LANES] for b in range(0, TILE, LANES)]
        base = [jnp.floor(r * (1.0 / span)) * span for r in row]
        best = [jnp.full((1, LANES), -1.0, F32) for _ in row]
        for j in range(i + 1):
            at = slice(j * TILE, (j + 1) * TILE)
            scores = dot_t(tile(j), mine)
            col, low = col_scr[at, :], base_scr[at, :]
            across = across_scr[at, :]
            for b in range(len(row)):
                part = scores[:, b * LANES : (b + 1) * LANES]
                kept = jnp.where((col < row[b]) & (col >= base[b]), part, -1.0)
                best[b] = jnp.maximum(best[b], jnp.max(kept, axis=0, keepdims=True))
                if j < i:
                    across = jnp.maximum(across, jnp.where((row[b] < col) & (row[b] >= low), part, -1.0))
            if j < i:
                across_scr[at, :] = across
        down += best

    best = [
        jnp.maximum(
            down[b], jnp.max(across_scr[b * LANES : (b + 1) * LANES, :].T, axis=0, keepdims=True)
        )
        for b in range(rows // LANES)
    ]
    best = jnp.concatenate(best, axis=1)
    homes = out_ref.shape[0]
    place_in = iota((1, rows), 1)
    slot = place_in // TILE
    plane = place_in % TILE // per_pair
    shift = jnp.zeros((1, rows), I32)
    for t, dz in enumerate(ORDER):
        shift = jnp.where(slot == t, dz, shift)
    z = (my_z() + NZ - shift) % NZ
    home = plane // CORES * (CORES * NZ) + z * CORES + plane % CORES
    to = (iota((homes, rows), 0) == home).astype(BF16)
    own = iota((per_pair, rows), 0) == place_in % per_pair
    rest = jnp.where(own, best, 0.0)
    total = jnp.zeros(out_ref.shape, F32)
    for _ in range(3):
        part = rest.astype(BF16)
        rest = rest - part.astype(F32)
        total = total + dot_t(to, part)
    out_ref[...] = total


def home_kernel(ret_ref, pos_ref, out_ref):
    owners, per_pair = ret_ref.shape
    pos = wide_row(pos_ref)
    rows = pos.shape[1]
    owner = pos // per_pair
    rank = pos - owner * per_pair
    slot = (iota((per_pair, rows), 0) == rank).astype(BF16)
    rest = ret_ref[...]
    spread = jnp.zeros((owners, rows), F32)
    for _ in range(3):
        part = rest.astype(BF16)
        rest = rest - part.astype(F32)
        spread = spread + dot(part, slot)
    mine = jnp.where(iota((owners, rows), 0) == owner, spread, 0.0)
    put_row(out_ref, jnp.sum(mine, axis=0, keepdims=True))


def whole(shape):
    return pl.BlockSpec(shape, lambda *_: (0,) * len(shape))


ANY = pl.BlockSpec(memory_space=pl.ANY)
FIRST = pltpu.CompilerParams(vmem_limit_bytes=61 * 1024 * 1024)
LIMIT = pltpu.CompilerParams(vmem_limit_bytes=24 * 1024 * 1024)


def shape(dims, dtype):
    return jax.ShapeDtypeStruct(dims, dtype)


def cost(macs):
    return pl.CostEstimate(flops=2 * macs, bytes_accessed=8 << 20, transcendentals=0)


def to_shift(rows, dz):
    members = lax.axis_size("member")
    pairs = []
    for i in range(members):
        z = (i // CORES) % NZ
        pairs.append((i, i + ((z + dz) % NZ - z) * CORES))
    return lax.ppermute(rows, "member", pairs)


def in_plane(rows):
    members = lax.axis_size("member")
    groups = [[i for i in range(members) if (i // CORES) % NZ == z] for z in range(NZ)]
    return lax.all_to_all(rows, "member", split_axis=0, concat_axis=0, tiled=True, axis_index_groups=groups)


def step_of_its_own(run, flag, *args):
    kinds = jax.eval_shape(run, *args)
    skip = lambda *_: jax.tree.map(lambda kind: jnp.zeros(kind.shape, kind.dtype), kinds)
    return lax.cond(flag[0] > 0, run, skip, *args)


def on_device(embeds, cluster_id, row_index):
    members = lax.axis_size("member")
    rows, width = embeds.shape
    per_owner = CLUSTERS // members
    per_pair = rows // members
    lines = rows // LANES
    tall = width // LANES * per_pair + META
    block = (PLANE, tall, LANES)
    one, pos, meta, flag = pl.pallas_call(
        functools.partial(first_kernel, members, per_owner, per_pair),
        in_specs=[ANY, ANY, ANY],
        out_specs=[whole(block), whole((lines, LANES)), whole((members, LANES)), pl.BlockSpec(memory_space=pltpu.SMEM)],
        out_shape=[
            shape(block, BF16),
            shape((lines, LANES), I32),
            shape((members, LANES), F32),
            shape((1,), I32),
        ],
        scratch_shapes=[
            pltpu.VMEM((lines, LANES), I32),
            pltpu.VMEM((lines, LANES), I32),
            pltpu.VMEM((rows, width), BF16),
            pltpu.SemaphoreType.DMA((3,)),
        ],
        compiler_params=FIRST,
        cost_estimate=cost(TILE * rows * width),
        name="send_first",
    )(cluster_id.reshape(lines, LANES), row_index.reshape(lines, LANES), embeds)
    got = [to_shift(one, EARLY[0])]

    def send_some(shifts, name, pos, meta, embeds):
        return pl.pallas_call(
            functools.partial(some_kernel, per_pair, shifts),
            in_specs=[whole((lines, LANES)), whole((members, LANES)), ANY],
            out_shape=[shape(block, BF16) for _ in shifts],
            scratch_shapes=[pltpu.VMEM((rows, width), BF16), pltpu.SemaphoreType.DMA],
            compiler_params=LIMIT,
            cost_estimate=cost(len(shifts) * TILE * rows * width),
            name=name,
        )(pos, meta, embeds)

    more = send_some(EARLY[1:-1], "send_early", pos, meta, embeds)
    got += [to_shift(x, dz) for x, dz in zip(more, EARLY[1:-1])]

    def late_part(pos, meta, embeds):
        steps = 4
        late = pl.pallas_call(
            functools.partial(late_kernel, per_pair),
            grid=(steps,),
            in_specs=[whole((lines, LANES)), whole((members, LANES)), ANY],
            out_specs=pl.BlockSpec((PLANE // steps, len(LATE), tall, LANES), lambda s: (s, 0, 0, 0)),
            out_shape=shape((PLANE, len(LATE), tall, LANES), BF16),
            scratch_shapes=[
                pltpu.VMEM((rows, width), BF16),
                pltpu.VMEM((1, rows), I32),
                pltpu.SemaphoreType.DMA,
            ],
            compiler_params=LIMIT,
            cost_estimate=cost(len(LATE) * TILE * rows * width),
            name="send_late",
        )(pos, meta, embeds)
        late = in_plane(late)
        return [late[:, k] for k in range(len(LATE))] + list(
            send_some(EARLY[-1:], "send_own", pos, meta, embeds)
        )

    *moving, own = step_of_its_own(late_part, flag, pos, meta, embeds)
    shifted = [to_shift(x, dz) for x, dz in zip(moving, LATE)]
    early = step_of_its_own(lambda *got: in_plane(jnp.stack(got, axis=1)), flag, *got, own)
    best = pl.pallas_call(
        functools.partial(best_kernel, per_pair),
        out_shape=shape((members, per_pair), F32),
        scratch_shapes=[
            pltpu.VMEM((rows, LANES), F32),
            pltpu.VMEM((rows, LANES), F32),
            pltpu.VMEM((8, rows), F32),
            pltpu.VMEM((rows, LANES), F32),
        ],
        compiler_params=LIMIT,
        cost_estimate=cost(rows * rows * width // 2),
        name="best",
    )(early, *shifted)
    back = lax.all_to_all(best, "member", split_axis=0, concat_axis=0, tiled=True)
    nearest = pl.pallas_call(
        home_kernel,
        out_shape=shape((lines, LANES), F32),
        compiler_params=LIMIT,
        name="home",
    )(back, pos)
    return nearest.reshape(rows)


def solution(mesh):
    in_specs = (P(("outer", "member"), None), P(("outer", "member")), P(("outer", "member")))
    out_specs = P(("outer", "member"))
    return jax.shard_map(
        on_device, mesh=mesh, in_specs=in_specs, out_specs=out_specs, check_vma=False
    )
```

```python
import functools

import jax
import jax.numpy as jnp
from jax import lax
from jax.experimental import pallas as pl
from jax.experimental.pallas import tpu as pltpu
from jax.sharding import PartitionSpec as P

CLUSTERS = 256
INDEX_BITS = 17
LANES = 128
META = 8
TILE = 256
NZ, CORES, PLANE = 8, 2, 8
EARLY = (4, 3, 5, 0)
LATE = (2, 6, 1, 7)
ORDER = EARLY + LATE
BF16, F32, I32 = jnp.bfloat16, jnp.float32, jnp.int32


def iota(shape, dim):
    return lax.broadcasted_iota(I32, shape, dim)


def dot(a, b):
    return jnp.dot(a, b, preferred_element_type=F32)


def dot_t(a, b):
    return lax.dot_general(a, b, (((1,), (1,)), ((), ())), preferred_element_type=F32)


def wide_row(ref):
    return jnp.concatenate([ref[b : b + 1, :] for b in range(ref.shape[0])], axis=1)


def put_row(ref, row):
    for b in range(ref.shape[0]):
        ref[b : b + 1, :] = row[:, b * LANES : (b + 1) * LANES]


def my_z():
    return (lax.axis_index("member") // CORES) % NZ


def shift_plane(owner):
    dz = ((owner // CORES) % NZ + NZ - my_z()) % NZ
    return dz, owner // (CORES * NZ) * CORES + owner % CORES


def route(owners, per_owner, per_pair, cid, idx):
    rows = cid.shape[1]
    owner = cid // per_owner
    dz, plane = shift_plane(owner)
    hot = (iota((owners, rows), 0) == dz * PLANE + plane).astype(BF16)
    before = (iota((TILE, TILE), 0) < iota((TILE, TILE), 1)).astype(BF16)
    carry = jnp.zeros((owners, 1), F32)
    ranks = []
    for b in range(rows // TILE):
        part = hot[:, b * TILE : (b + 1) * TILE]
        wide = part.astype(F32)
        ranks.append(jnp.sum((dot(part, before) + carry) * wide, axis=0, keepdims=True))
        carry = carry + jnp.sum(wide, axis=1, keepdims=True)
    rank = jnp.concatenate(ranks, axis=1).astype(I32)
    key = (cid - owner * per_owner) * (1 << INDEX_BITS) + idx
    slot = iota((per_pair, rows), 0) == rank
    pieces = (key & 255, (key >> 8) & 255, key >> 16)
    spread = [jnp.where(slot, p.astype(F32), 0.0).astype(BF16) for p in pieces]
    spread.append(jnp.zeros((LANES - 3 * per_pair, rows), BF16))
    meta = dot_t(hot, jnp.concatenate(spread, axis=0))
    return owner * per_pair + rank, meta


def place(pos, per_pair, shifts, inner):
    owner = pos // per_pair
    rank = pos - owner * per_pair
    dz, plane = shift_plane(owner)
    goal = jnp.full(pos.shape, -1, I32)
    for k, shift in enumerate(shifts):
        slot = plane * len(shifts) + k if inner else k * PLANE + plane
        goal = jnp.where(dz == shift, slot * per_pair + rank, goal)
    return goal


def scaled(moved):
    inverse = lax.rsqrt(jnp.sum(moved * moved, axis=1, keepdims=True) + 1e-06)
    return (moved * inverse).astype(BF16)


def picked(goal, first, size):
    return (iota((size, goal.shape[1]), 0) + first == goal).astype(BF16)


def put_pair(ref, at, unit):
    rows = unit.shape[0]
    for c in range(unit.shape[1] // LANES):
        ref[at + c * rows : at + (c + 1) * rows, :] = unit[:, c * LANES : (c + 1) * LANES]


def put_block(ref, unit, meta):
    rows = unit.shape[0] // PLANE
    tall = ref.shape[0] // PLANE - 1
    for p in range(PLANE):
        put_pair(ref, p * tall, unit[p * rows : (p + 1) * rows])
    ref[PLANE * tall :, :] = meta.astype(BF16)


def first_kernel(
    owners, per_owner, per_pair, cid_hbm, idx_hbm, emb_hbm, out_ref, pos_ref, meta_ref, flag_ref,
    cid_ref, idx_ref, emb_ref, sem
):
    copies = [
        pltpu.make_async_copy(src, dst, sem.at[n])
        for n, (src, dst) in enumerate(((cid_hbm, cid_ref), (idx_hbm, idx_ref), (emb_hbm, emb_ref)))
    ]
    for copy in copies:
        copy.start()
    copies[0].wait()
    copies[1].wait()
    pos, meta = route(owners, per_owner, per_pair, wide_row(cid_ref), wide_row(idx_ref))
    put_row(pos_ref, pos)
    meta_ref[...] = meta
    flag_ref[0] = 1
    pick = picked(place(pos, per_pair, EARLY[:1], False), 0, PLANE * per_pair)
    copies[2].wait()
    shift = EARLY[0]
    put_block(out_ref, scaled(dot(pick, emb_ref[...])), meta[shift * PLANE : (shift + 1) * PLANE])


def some_kernel(per_pair, shifts, pos_ref, meta_ref, emb_ref, *outs):
    size = PLANE * per_pair
    goal = place(wide_row(pos_ref), per_pair, shifts, False)
    unit = scaled(dot(picked(goal, 0, size * len(outs)), emb_ref[...]))
    for k, (shift, out_ref) in enumerate(zip(shifts, outs)):
        put_block(out_ref, unit[k * size : (k + 1) * size], meta_ref[shift * PLANE : (shift + 1) * PLANE, :])


def late_kernel(per_pair, _, pos_ref, meta_ref, emb_ref, late_ref):
    goal = place(wide_row(pos_ref), per_pair, LATE, True)
    some = len(LATE) * per_pair
    tall = emb_ref.shape[1] // LANES * per_pair
    step = 512 // some
    for p0 in range(0, PLANE, step):
        unit = scaled(dot(picked(goal, p0 * some, step * some), emb_ref[...]))
        for p in range(p0, p0 + step):
            for k in range(len(LATE)):
                at = ((p - p0) * len(LATE) + k) * per_pair
                put_pair(late_ref.at[p], k * tall, unit[at : at + per_pair])
            meta = [meta_ref[shift * PLANE + p : shift * PLANE + p + 1, :] for shift in LATE]
            meta.append(jnp.zeros((META - len(LATE), LANES), F32))
            late_ref[p, len(LATE) * tall :, :] = jnp.concatenate(meta, axis=0).astype(BF16)


def cut_kernel(got_ref, *outs):
    tall = outs[0].shape[0] // PLANE - 1
    meta = got_ref[:, len(outs) * tall :, :].astype(F32)
    for k, out_ref in enumerate(outs):
        for p in range(PLANE):
            out_ref[p * tall : (p + 1) * tall, :] = got_ref[p, k * tall : (k + 1) * tall, :]
        out_ref[PLANE * tall :, :] = meta[:, k, :].astype(BF16)


def merge_kernel(*refs):
    *ins, out_ref = refs
    tall = ins[0].shape[0] // PLANE - 1
    metas = [ref[PLANE * tall :, :].astype(F32) for ref in ins]
    for p in range(PLANE):
        for k, ref in enumerate(ins):
            out_ref[p, k * tall : (k + 1) * tall, :] = ref[p * tall : (p + 1) * tall, :]
        meta = [m[p : p + 1, :] for m in metas] + [jnp.zeros((META - len(ins), LANES), F32)]
        out_ref[p, len(ins) * tall :, :] = jnp.concatenate(meta, axis=0).astype(BF16)


def piece_weights(lane, per_pair):
    piece = lane // per_pair
    value = jnp.where(piece == 0, 1.0, jnp.where(piece == 1, 256.0, jnp.where(piece == 2, 65536.0, 0.0)))
    return value.astype(BF16)


def best_kernel(per_pair, early_ref, *refs):
    *late, out_ref, col_scr, group_scr, row_scr, across_scr = refs
    rows = col_scr.shape[0]
    tall = late[0].shape[0] // PLANE - 1
    chunks = tall // per_pair
    span = float(1 << INDEX_BITS)

    def pairs(t, at):
        if t < len(EARLY):
            return early_ref[:, t * tall + at : t * tall + at + per_pair, :].reshape(TILE, LANES)
        ref = late[t - len(EARLY)]
        return jnp.concatenate(
            [ref[p * tall + at : p * tall + at + per_pair, :] for p in range(PLANE)], axis=0
        )

    def tile(t):
        return jnp.concatenate([pairs(t, c * per_pair) for c in range(chunks)], axis=1)

    meta = early_ref[:, len(EARLY) * tall :, :].astype(F32)
    meta = [meta[:, k, :] for k in range(len(EARLY))] + [ref[PLANE * tall :, :].astype(F32) for ref in late]
    meta = jnp.concatenate(meta, axis=0)[:, None, :]
    meta = jnp.broadcast_to(meta, (rows // per_pair, per_pair, LANES)).reshape(rows, LANES)
    own = (iota((rows, LANES), 0) % per_pair) == (iota((rows, LANES), 1) % per_pair)
    meta = jnp.where(own, meta, 0.0).astype(BF16)
    col = dot(meta, piece_weights(iota((LANES, LANES), 0), per_pair))
    col_scr[...] = col
    group_scr[...] = jnp.floor(col * (1.0 / span))
    row_scr[...] = dot_t(piece_weights(iota((8, LANES), 1), per_pair), meta)
    across_scr[...] = jnp.full(across_scr.shape, -1.0, F32)

    down = []
    for i in range(rows // TILE):
        mine = tile(i)
        row = [row_scr[0:1, i * TILE + b : i * TILE + b + LANES] for b in range(0, TILE, LANES)]
        group = [jnp.floor(r * (1.0 / span)) for r in row]
        best = [jnp.full((1, LANES), -1.0, F32) for _ in row]
        for j in range(i + 1):
            at = slice(j * TILE, (j + 1) * TILE)
            scores = dot_t(tile(j), mine)
            col, col_group = col_scr[at, :], group_scr[at, :]
            across = across_scr[at, :]
            for b in range(len(row)):
                part = jnp.where(col_group == group[b], scores[:, b * LANES : (b + 1) * LANES], -1.0)
                before = col < row[b]
                best[b] = jnp.maximum(best[b], jnp.max(jnp.where(before, part, -1.0), axis=0, keepdims=True))
                if j < i:
                    across = jnp.maximum(across, jnp.where(before, -1.0, part))
            if j < i:
                across_scr[at, :] = across
        down += best

    best = [
        jnp.maximum(
            down[b], jnp.max(across_scr[b * LANES : (b + 1) * LANES, :].T, axis=0, keepdims=True)
        )
        for b in range(rows // LANES)
    ]
    best = jnp.concatenate(best, axis=1)
    homes = out_ref.shape[0]
    place_in = iota((1, rows), 1)
    slot = place_in // TILE
    plane = place_in % TILE // per_pair
    shift = jnp.zeros((1, rows), I32)
    for t, dz in enumerate(ORDER):
        shift = jnp.where(slot == t, dz, shift)
    z = (my_z() + NZ - shift) % NZ
    home = plane // CORES * (CORES * NZ) + z * CORES + plane % CORES
    to = (iota((homes, rows), 0) == home).astype(BF16)
    own = iota((per_pair, rows), 0) == place_in % per_pair
    rest = jnp.where(own, best, 0.0)
    total = jnp.zeros(out_ref.shape, F32)
    for _ in range(3):
        part = rest.astype(BF16)
        rest = rest - part.astype(F32)
        total = total + dot_t(to, part)
    out_ref[...] = total


def home_kernel(ret_ref, pos_ref, out_ref):
    owners, per_pair = ret_ref.shape
    pos = wide_row(pos_ref)
    rows = pos.shape[1]
    owner = pos // per_pair
    rank = pos - owner * per_pair
    slot = (iota((per_pair, rows), 0) == rank).astype(BF16)
    rest = ret_ref[...]
    spread = jnp.zeros((owners, rows), F32)
    for _ in range(3):
        part = rest.astype(BF16)
        rest = rest - part.astype(F32)
        spread = spread + dot(part, slot)
    mine = jnp.where(iota((owners, rows), 0) == owner, spread, 0.0)
    put_row(out_ref, jnp.sum(mine, axis=0, keepdims=True))


def whole(shape):
    return pl.BlockSpec(shape, lambda *_: (0,) * len(shape))


ANY = pl.BlockSpec(memory_space=pl.ANY)
VMEM = pl.BlockSpec(memory_space=pltpu.VMEM)
FIRST = pltpu.CompilerParams(vmem_limit_bytes=61 * 1024 * 1024)
LIMIT = pltpu.CompilerParams(vmem_limit_bytes=24 * 1024 * 1024)


def shape(dims, dtype):
    return jax.ShapeDtypeStruct(dims, dtype)


def cost(macs):
    return pl.CostEstimate(flops=2 * macs, bytes_accessed=8 << 20, transcendentals=0)


def to_shift(rows, dz):
    members = lax.axis_size("member")
    pairs = []
    for i in range(members):
        z = (i // CORES) % NZ
        pairs.append((i, i + ((z + dz) % NZ - z) * CORES))
    return lax.ppermute(rows, "member", pairs)


def in_plane(rows):
    members = lax.axis_size("member")
    groups = [[i for i in range(members) if (i // CORES) % NZ == z] for z in range(NZ)]
    return lax.all_to_all(rows, "member", split_axis=0, concat_axis=0, tiled=True, axis_index_groups=groups)


def step_of_its_own(run, flag, *args):
    kinds = jax.eval_shape(run, *args)
    skip = lambda *_: jax.tree.map(lambda kind: jnp.zeros(kind.shape, kind.dtype), kinds)
    return lax.cond(flag[0] > 0, run, skip, *args)


def on_device(embeds, cluster_id, row_index):
    members = lax.axis_size("member")
    rows, width = embeds.shape
    per_owner = CLUSTERS // members
    per_pair = rows // members
    lines = rows // LANES
    tall = width // LANES * per_pair
    block = (PLANE * (tall + 1), LANES)
    one, pos, meta, flag = pl.pallas_call(
        functools.partial(first_kernel, members, per_owner, per_pair),
        in_specs=[ANY, ANY, ANY],
        out_specs=[whole(block), whole((lines, LANES)), whole((members, LANES)), pl.BlockSpec(memory_space=pltpu.SMEM)],
        out_shape=[
            shape(block, BF16),
            shape((lines, LANES), I32),
            shape((members, LANES), F32),
            shape((1,), I32),
        ],
        scratch_shapes=[
            pltpu.VMEM((lines, LANES), I32),
            pltpu.VMEM((lines, LANES), I32),
            pltpu.VMEM((rows, width), BF16),
            pltpu.SemaphoreType.DMA((3,)),
        ],
        compiler_params=FIRST,
        cost_estimate=cost(TILE * rows * width),
        name="send_first",
    )(cluster_id.reshape(lines, LANES), row_index.reshape(lines, LANES), embeds)
    got = [to_shift(one, EARLY[0])]

    def send(kernel, shifts, more, name):
        return pl.pallas_call(
            functools.partial(kernel, per_pair, shifts),
            in_specs=[whole((lines, LANES)), whole((members, LANES)), VMEM],
            out_shape=[shape(block, BF16) for _ in shifts] + more,
            compiler_params=LIMIT,
            cost_estimate=cost(len(shifts) * TILE * rows * width),
            name=name,
        )

    more = send(some_kernel, EARLY[1:3], [], "send_early")(pos, meta, embeds)
    got += [to_shift(x, dz) for x, dz in zip(more, EARLY[1:3])]

    def late_part(pos, meta, embeds):
        late = send(late_kernel, (), [shape((PLANE, len(LATE) * tall + META, LANES), BF16)], "send_late")
        late = in_plane(late(pos, meta, embeds)[0])
        parts = pl.pallas_call(
            cut_kernel, out_shape=[shape(block, BF16) for _ in LATE], compiler_params=LIMIT, name="cut"
        )(late)
        return parts + send(some_kernel, (0,), [], "send_own")(pos, meta, embeds)

    *moving, own = step_of_its_own(late_part, flag, pos, meta, embeds)
    shifted = [to_shift(x, dz) for x, dz in zip(moving, LATE)]

    def last_part(got):
        early = pl.pallas_call(
            merge_kernel,
            out_shape=shape((PLANE, len(got) * tall + META, LANES), BF16),
            compiler_params=LIMIT,
            name="merge",
        )(*got)
        return in_plane(early)

    early = step_of_its_own(last_part, flag, got + [own])
    best = pl.pallas_call(
        functools.partial(best_kernel, per_pair),
        out_shape=shape((members, per_pair), F32),
        scratch_shapes=[
            pltpu.VMEM((rows, LANES), F32),
            pltpu.VMEM((rows, LANES), F32),
            pltpu.VMEM((8, rows), F32),
            pltpu.VMEM((rows, LANES), F32),
        ],
        compiler_params=LIMIT,
        cost_estimate=cost(rows * rows * width // 2),
        name="best",
    )(early, *shifted)
    back = lax.all_to_all(best, "member", split_axis=0, concat_axis=0, tiled=True)
    nearest = pl.pallas_call(
        home_kernel,
        out_shape=shape((lines, LANES), F32),
        compiler_params=LIMIT,
        name="home",
    )(back, pos)
    return nearest.reshape(rows)


def solution(mesh):
    in_specs = (P(("outer", "member"), None), P(("outer", "member")), P(("outer", "member")))
    out_specs = P(("outer", "member"))
    return jax.shard_map(
        on_device, mesh=mesh, in_specs=in_specs, out_specs=out_specs, check_vma=False
    )
```

```python
import functools

import jax
import jax.numpy as jnp
from jax import lax
from jax.experimental import pallas as pl
from jax.experimental.pallas import tpu as pltpu
from jax.sharding import PartitionSpec as P

CLUSTERS = 256
INDEX_BITS = 17
LANES = 128
META = 8
TILE = 256
NZ, CORES, PLANE = 8, 2, 8
EARLY = (4, 3, 5, 0)
LATE = (2, 6, 1, 7)
SOON, NEXT = (4,), (3, 5, 0)
ORDER = LATE + EARLY
BF16, F32, I32 = jnp.bfloat16, jnp.float32, jnp.int32


def iota(shape, dim):
    return lax.broadcasted_iota(I32, shape, dim)


def dot(a, b):
    return jnp.dot(a, b, preferred_element_type=F32)


def dot_t(a, b):
    return lax.dot_general(a, b, (((1,), (1,)), ((), ())), preferred_element_type=F32)


def wide_row(ref):
    return jnp.concatenate([ref[b : b + 1, :] for b in range(ref.shape[0])], axis=1)


def put_row(ref, row):
    for b in range(ref.shape[0]):
        ref[b : b + 1, :] = row[:, b * LANES : (b + 1) * LANES]


def my_z():
    return (lax.axis_index("member") // CORES) % NZ


def shift_plane(owner):
    dz = ((owner // CORES) % NZ + NZ - my_z()) % NZ
    return dz, owner // (CORES * NZ) * CORES + owner % CORES


def route(owners, per_owner, per_pair, cid, idx):
    rows = cid.shape[1]
    owner = cid // per_owner
    dz, plane = shift_plane(owner)
    hot = (iota((owners, rows), 0) == dz * PLANE + plane).astype(BF16)
    before = (iota((TILE, TILE), 0) < iota((TILE, TILE), 1)).astype(BF16)
    carry = jnp.zeros((owners, 1), F32)
    ranks = []
    for b in range(rows // TILE):
        part = hot[:, b * TILE : (b + 1) * TILE]
        wide = part.astype(F32)
        ranks.append(jnp.sum((dot(part, before) + carry) * wide, axis=0, keepdims=True))
        carry = carry + jnp.sum(wide, axis=1, keepdims=True)
    rank = jnp.concatenate(ranks, axis=1).astype(I32)
    key = (cid - owner * per_owner) * (1 << INDEX_BITS) + idx
    slot = iota((per_pair, rows), 0) == rank
    pieces = (key & 255, (key >> 8) & 255, key >> 16)
    spread = [jnp.where(slot, p.astype(F32), 0.0).astype(BF16) for p in pieces]
    spread.append(jnp.zeros((LANES - 3 * per_pair, rows), BF16))
    meta = dot_t(hot, jnp.concatenate(spread, axis=0))
    return owner * per_pair + rank, meta


def place(pos, per_pair, shifts, inner):
    owner = pos // per_pair
    rank = pos - owner * per_pair
    dz, plane = shift_plane(owner)
    goal = jnp.full(pos.shape, -1, I32)
    for k, shift in enumerate(shifts):
        slot = plane * len(shifts) + k if inner else k * PLANE + plane
        goal = jnp.where(dz == shift, slot * per_pair + rank, goal)
    return goal


def scaled(moved):
    inverse = lax.rsqrt(jnp.sum(moved * moved, axis=1, keepdims=True) + 1e-06)
    return (moved * inverse).astype(BF16)


def picked(goal, first, size):
    return (iota((size, goal.shape[1]), 0) + first == goal).astype(BF16)


def put_pair(ref, at, unit):
    rows = unit.shape[0]
    for c in range(unit.shape[1] // LANES):
        ref[at + c * rows : at + (c + 1) * rows, :] = unit[:, c * LANES : (c + 1) * LANES]


def put_block(ref, unit, meta):
    rows = unit.shape[0] // PLANE
    tall = ref.shape[0] // PLANE - 1
    for p in range(PLANE):
        put_pair(ref, p * tall, unit[p * rows : (p + 1) * rows])
    ref[PLANE * tall :, :] = meta.astype(BF16)


def put_blocks(outs, shifts, goal, meta_ref, emb_ref, per_pair):
    size = PLANE * per_pair
    unit = scaled(dot(picked(goal, 0, size * len(outs)), emb_ref[...]))
    for k, (shift, out_ref) in enumerate(zip(shifts, outs)):
        put_block(out_ref, unit[k * size : (k + 1) * size], meta_ref[shift * PLANE : (shift + 1) * PLANE, :])


def first_kernel(owners, per_owner, per_pair, cid_hbm, idx_hbm, emb_hbm, *refs):
    *outs, pos_ref, meta_ref, flag_ref, emb_ref, cid_ref, idx_ref, sem = refs
    copies = [
        pltpu.make_async_copy(src, dst, sem.at[n])
        for n, (src, dst) in enumerate(((cid_hbm, cid_ref), (idx_hbm, idx_ref), (emb_hbm, emb_ref)))
    ]
    for copy in copies:
        copy.start()
    copies[0].wait()
    copies[1].wait()
    pos, meta = route(owners, per_owner, per_pair, wide_row(cid_ref), wide_row(idx_ref))
    put_row(pos_ref, pos)
    meta_ref[...] = meta
    flag_ref[0] = 1
    goal = place(pos, per_pair, SOON, False)
    copies[2].wait()
    put_blocks(outs, SOON, goal, meta_ref, emb_ref, per_pair)


def some_kernel(per_pair, shifts, pos_ref, meta_ref, emb_ref, *outs):
    goal = place(wide_row(pos_ref), per_pair, shifts, False)
    put_blocks(outs, shifts, goal, meta_ref, emb_ref, per_pair)


def rest_kernel(per_pair, shifts, pos_ref, meta_ref, emb_ref, *refs):
    *outs, late_ref = refs
    some_kernel(per_pair, shifts, pos_ref, meta_ref, emb_ref, *outs)
    goal = place(wide_row(pos_ref), per_pair, LATE, True)
    some = len(LATE) * per_pair
    tall = emb_ref.shape[1] // LANES * per_pair
    step = 512 // some
    for p0 in range(0, PLANE, step):
        unit = scaled(dot(picked(goal, p0 * some, step * some), emb_ref[...]))
        for p in range(p0, p0 + step):
            for k in range(len(LATE)):
                at = ((p - p0) * len(LATE) + k) * per_pair
                put_pair(late_ref.at[p], k * tall, unit[at : at + per_pair])
            meta = [meta_ref[shift * PLANE + p : shift * PLANE + p + 1, :] for shift in LATE]
            meta.append(jnp.zeros((META - len(LATE), LANES), F32))
            late_ref[p, len(LATE) * tall :, :] = jnp.concatenate(meta, axis=0).astype(BF16)


def cut_kernel(got_ref, *outs):
    tall = outs[0].shape[0] // PLANE - 1
    meta = got_ref[:, len(outs) * tall :, :].astype(F32)
    for k, out_ref in enumerate(outs):
        for p in range(PLANE):
            out_ref[p * tall : (p + 1) * tall, :] = got_ref[p, k * tall : (k + 1) * tall, :]
        out_ref[PLANE * tall :, :] = meta[:, k, :].astype(BF16)


def merge_kernel(*refs):
    *ins, out_ref = refs
    tall = ins[0].shape[0] // PLANE - 1
    metas = [ref[PLANE * tall :, :].astype(F32) for ref in ins]
    for p in range(PLANE):
        for k, ref in enumerate(ins):
            out_ref[p, k * tall : (k + 1) * tall, :] = ref[p * tall : (p + 1) * tall, :]
        meta = [m[p : p + 1, :] for m in metas] + [jnp.zeros((META - len(ins), LANES), F32)]
        out_ref[p, len(ins) * tall :, :] = jnp.concatenate(meta, axis=0).astype(BF16)


def piece_weights(lane, per_pair):
    piece = lane // per_pair
    value = jnp.where(piece == 0, 1.0, jnp.where(piece == 1, 256.0, jnp.where(piece == 2, 65536.0, 0.0)))
    return value.astype(BF16)


def best_kernel(per_pair, early_hbm, *refs):
    *late, out_ref, early_ref, col_scr, group_scr, row_scr, across_scr, sem = refs
    copy = pltpu.make_async_copy(early_hbm, early_ref, sem)
    copy.start()
    rows = col_scr.shape[0]
    tall = late[0].shape[0] // PLANE - 1
    chunks = tall // per_pair
    span = float(1 << INDEX_BITS)

    def pairs(t, at):
        k = t - len(LATE)
        if k >= 0:
            return early_ref[:, k * tall + at : k * tall + at + per_pair, :].reshape(TILE, LANES)
        return jnp.concatenate(
            [late[t][p * tall + at : p * tall + at + per_pair, :] for p in range(PLANE)], axis=0
        )

    def tile(t):
        return jnp.concatenate([pairs(t, c * per_pair) for c in range(chunks)], axis=1)

    def keys(first, metas):
        size = len(metas) * TILE
        at = slice(first * TILE, first * TILE + size)
        meta = jnp.concatenate(metas, axis=0)[:, None, :]
        meta = jnp.broadcast_to(meta, (size // per_pair, per_pair, LANES)).reshape(size, LANES)
        own = (iota((size, LANES), 0) % per_pair) == (iota((size, LANES), 1) % per_pair)
        meta = jnp.where(own, meta, 0.0).astype(BF16)
        col = dot(meta, piece_weights(iota((LANES, LANES), 0), per_pair))
        col_scr[at, :] = col
        group_scr[at, :] = jnp.floor(col * (1.0 / span))
        row_scr[:, at] = dot_t(piece_weights(iota((8, LANES), 1), per_pair), meta)
        across_scr[at, :] = jnp.full((size, LANES), -1.0, F32)

    keys(0, [ref[PLANE * tall :, :].astype(F32) for ref in late])
    down = []
    for i in range(rows // TILE):
        if i == len(LATE):
            copy.wait()
            meta = early_ref[:, len(EARLY) * tall :, :].astype(F32)
            keys(i, [meta[:, k, :] for k in range(len(EARLY))])
        mine = tile(i)
        row = [row_scr[0:1, i * TILE + b : i * TILE + b + LANES] for b in range(0, TILE, LANES)]
        group = [jnp.floor(r * (1.0 / span)) for r in row]
        best = [jnp.full((1, LANES), -1.0, F32) for _ in row]
        for j in range(i + 1):
            at = slice(j * TILE, (j + 1) * TILE)
            scores = dot_t(tile(j), mine)
            col, col_group = col_scr[at, :], group_scr[at, :]
            across = across_scr[at, :]
            for b in range(len(row)):
                part = jnp.where(col_group == group[b], scores[:, b * LANES : (b + 1) * LANES], -1.0)
                before = col < row[b]
                best[b] = jnp.maximum(best[b], jnp.max(jnp.where(before, part, -1.0), axis=0, keepdims=True))
                if j < i:
                    across = jnp.maximum(across, jnp.where(before, -1.0, part))
            if j < i:
                across_scr[at, :] = across
        down += best

    best = [
        jnp.maximum(
            down[b], jnp.max(across_scr[b * LANES : (b + 1) * LANES, :].T, axis=0, keepdims=True)
        )
        for b in range(rows // LANES)
    ]
    best = jnp.concatenate(best, axis=1)
    homes = out_ref.shape[0]
    place_in = iota((1, rows), 1)
    slot = place_in // TILE
    plane = place_in % TILE // per_pair
    shift = jnp.zeros((1, rows), I32)
    for t, dz in enumerate(ORDER):
        shift = jnp.where(slot == t, dz, shift)
    z = (my_z() + NZ - shift) % NZ
    home = plane // CORES * (CORES * NZ) + z * CORES + plane % CORES
    to = (iota((homes, rows), 0) == home).astype(BF16)
    own = iota((per_pair, rows), 0) == place_in % per_pair
    rest = jnp.where(own, best, 0.0)
    total = jnp.zeros(out_ref.shape, F32)
    for _ in range(3):
        part = rest.astype(BF16)
        rest = rest - part.astype(F32)
        total = total + dot_t(to, part)
    out_ref[...] = total


def home_kernel(ret_ref, pos_ref, out_ref):
    owners, per_pair = ret_ref.shape
    pos = wide_row(pos_ref)
    rows = pos.shape[1]
    owner = pos // per_pair
    rank = pos - owner * per_pair
    slot = (iota((per_pair, rows), 0) == rank).astype(BF16)
    rest = ret_ref[...]
    spread = jnp.zeros((owners, rows), F32)
    for _ in range(3):
        part = rest.astype(BF16)
        rest = rest - part.astype(F32)
        spread = spread + dot(part, slot)
    mine = jnp.where(iota((owners, rows), 0) == owner, spread, 0.0)
    put_row(out_ref, jnp.sum(mine, axis=0, keepdims=True))


def whole(shape):
    return pl.BlockSpec(shape, lambda *_: (0,) * len(shape))


ANY = pl.BlockSpec(memory_space=pl.ANY)
VMEM = pl.BlockSpec(memory_space=pltpu.VMEM)
LIMIT = pltpu.CompilerParams(vmem_limit_bytes=24 * 1024 * 1024)


def in_hbm(*arrays):
    return [pltpu.with_memory_space_constraint(x, pltpu.HBM) for x in arrays]


def shape(dims, dtype):
    return jax.ShapeDtypeStruct(dims, dtype)


def cost(macs):
    return pl.CostEstimate(flops=2 * macs, bytes_accessed=8 << 20, transcendentals=0)


def to_shift(rows, dz):
    members = lax.axis_size("member")
    pairs = []
    for i in range(members):
        z = (i // CORES) % NZ
        pairs.append((i, i + ((z + dz) % NZ - z) * CORES))
    return lax.ppermute(rows, "member", pairs)


def in_plane(rows):
    members = lax.axis_size("member")
    groups = [[i for i in range(members) if (i // CORES) % NZ == z] for z in range(NZ)]
    return lax.all_to_all(rows, "member", split_axis=0, concat_axis=0, tiled=True, axis_index_groups=groups)


def step_of_its_own(run, flag, *args):
    kinds = jax.eval_shape(run, *args)
    skip = lambda *_: jax.tree.map(lambda kind: jnp.zeros(kind.shape, kind.dtype), kinds)
    return lax.cond(flag[0] > 0, run, skip, *args)


def on_device(embeds, cluster_id, row_index):
    members = lax.axis_size("member")
    rows, width = embeds.shape
    per_owner = CLUSTERS // members
    per_pair = rows // members
    lines = rows // LANES
    tall = width // LANES * per_pair
    block = (PLANE * (tall + 1), LANES)
    *parts, pos, meta, flag, kept = pl.pallas_call(
        functools.partial(first_kernel, members, per_owner, per_pair),
        in_specs=[ANY, ANY, ANY],
        out_specs=[whole(block) for _ in SOON]
        + [whole((lines, LANES)), whole((members, LANES)), pl.BlockSpec(memory_space=pltpu.SMEM), VMEM],
        out_shape=[shape(block, BF16) for _ in SOON]
        + [
            shape((lines, LANES), I32),
            shape((members, LANES), F32),
            shape((1,), I32),
            pltpu.VMEM((rows, width), BF16),
        ],
        scratch_shapes=[
            pltpu.VMEM((lines, LANES), I32),
            pltpu.VMEM((lines, LANES), I32),
            pltpu.SemaphoreType.DMA((3,)),
        ],
        compiler_params=LIMIT,
        cost_estimate=cost(TILE * rows * width),
        name="send_first",
    )(*in_hbm(cluster_id.reshape(lines, LANES), row_index.reshape(lines, LANES), embeds))
    got = {dz: to_shift(x, dz) for x, dz in zip(parts, SOON)}

    def send(kernel, shifts, more, name):
        return pl.pallas_call(
            functools.partial(kernel, per_pair, shifts),
            in_specs=[whole((lines, LANES)), whole((members, LANES)), VMEM],
            out_shape=[shape(block, BF16) for _ in shifts] + more,
            compiler_params=LIMIT,
            cost_estimate=cost(len(shifts) * TILE * rows * width),
            name=name,
        )

    *parts, late = send(
        rest_kernel, NEXT, [shape((PLANE, len(LATE) * tall + META, LANES), BF16)], "send_rest"
    )(pos, meta, kept)
    got |= {dz: to_shift(x, dz) if dz else x for x, dz in zip(parts, NEXT)}

    def late_part(late):
        late = in_plane(late)
        parts = pl.pallas_call(
            cut_kernel, out_shape=[shape(block, BF16) for _ in LATE], compiler_params=LIMIT, name="cut"
        )(late)
        return parts

    moving = step_of_its_own(late_part, flag, late)
    shifted = [to_shift(x, dz) for x, dz in zip(moving, LATE)]

    def last_part(got):
        early = pl.pallas_call(
            merge_kernel,
            out_shape=shape((PLANE, len(got) * tall + META, LANES), BF16),
            compiler_params=LIMIT,
            name="merge",
        )(*got)
        return in_plane(early)

    early = step_of_its_own(last_part, flag, [got[dz] for dz in EARLY])
    best = pl.pallas_call(
        functools.partial(best_kernel, per_pair),
        in_specs=[ANY] + [whole(block)] * len(LATE),
        out_shape=shape((members, per_pair), F32),
        scratch_shapes=[
            pltpu.VMEM((PLANE, len(EARLY) * tall + META, LANES), BF16),
            pltpu.VMEM((rows, LANES), F32),
            pltpu.VMEM((rows, LANES), F32),
            pltpu.VMEM((8, rows), F32),
            pltpu.VMEM((rows, LANES), F32),
            pltpu.SemaphoreType.DMA,
        ],
        compiler_params=LIMIT,
        cost_estimate=cost(rows * rows * width // 2),
        name="best",
    )(early, *shifted)
    back = lax.all_to_all(best, "member", split_axis=0, concat_axis=0, tiled=True)
    nearest = pl.pallas_call(
        home_kernel,
        out_shape=shape((lines, LANES), F32),
        compiler_params=LIMIT,
        name="home",
    )(back, pos)
    return nearest.reshape(rows)


def solution(mesh):
    in_specs = (P(("outer", "member"), None), P(("outer", "member")), P(("outer", "member")))
    out_specs = P(("outer", "member"))
    return jax.shard_map(
        on_device, mesh=mesh, in_specs=in_specs, out_specs=out_specs, check_vma=False
    )
```

```python
import functools

import jax
import jax.numpy as jnp
from jax import lax
from jax.experimental import pallas as pl
from jax.experimental.pallas import tpu as pltpu
from jax.sharding import PartitionSpec as P

CLUSTERS = 256
INDEX_BITS = 17
LANES = 128
META = 8
TILE = 256
NZ, CORES, PLANE = 8, 2, 8
EARLY = (4, 3, 5)
LATE = (2, 6, 1, 7, 0)
SOON, NEXT = (4,), (3, 5)
ORDER = (2, 6, 0, 4, 3, 5, 1, 7)
MID = range(3, 6)
BF16, F32, I32 = jnp.bfloat16, jnp.float32, jnp.int32


def iota(shape, dim):
    return lax.broadcasted_iota(I32, shape, dim)


def dot(a, b):
    return jnp.dot(a, b, preferred_element_type=F32)


def dot_t(a, b):
    return lax.dot_general(a, b, (((1,), (1,)), ((), ())), preferred_element_type=F32)


def wide_row(ref):
    return jnp.concatenate([ref[b : b + 1, :] for b in range(ref.shape[0])], axis=1)


def put_row(ref, row):
    for b in range(ref.shape[0]):
        ref[b : b + 1, :] = row[:, b * LANES : (b + 1) * LANES]


def my_z():
    return (lax.axis_index("member") // CORES) % NZ


def shift_plane(owner):
    dz = ((owner // CORES) % NZ + NZ - my_z()) % NZ
    return dz, owner // (CORES * NZ) * CORES + owner % CORES


def route(owners, per_owner, per_pair, cid, idx):
    rows = cid.shape[1]
    owner = cid // per_owner
    dz, plane = shift_plane(owner)
    hot = (iota((owners, rows), 0) == dz * PLANE + plane).astype(BF16)
    before = (iota((TILE, TILE), 0) < iota((TILE, TILE), 1)).astype(BF16)
    carry = jnp.zeros((owners, 1), F32)
    ranks = []
    for b in range(rows // TILE):
        part = hot[:, b * TILE : (b + 1) * TILE]
        wide = part.astype(F32)
        ranks.append(jnp.sum((dot(part, before) + carry) * wide, axis=0, keepdims=True))
        carry = carry + jnp.sum(wide, axis=1, keepdims=True)
    rank = jnp.concatenate(ranks, axis=1).astype(I32)
    key = (cid - owner * per_owner) * (1 << INDEX_BITS) + idx
    slot = iota((per_pair, rows), 0) == rank
    pieces = (key & 255, (key >> 8) & 255, key >> 16)
    spread = [jnp.where(slot, p.astype(F32), 0.0).astype(BF16) for p in pieces]
    spread.append(jnp.zeros((LANES - 3 * per_pair, rows), BF16))
    meta = dot_t(hot, jnp.concatenate(spread, axis=0))
    return owner * per_pair + rank, meta


def place(pos, per_pair, shifts, inner):
    owner = pos // per_pair
    rank = pos - owner * per_pair
    dz, plane = shift_plane(owner)
    goal = jnp.full(pos.shape, -1, I32)
    for k, shift in enumerate(shifts):
        slot = plane * len(shifts) + k if inner else k * PLANE + plane
        goal = jnp.where(dz == shift, slot * per_pair + rank, goal)
    return goal


def scaled(moved):
    inverse = lax.rsqrt(jnp.sum(moved * moved, axis=1, keepdims=True) + 1e-06)
    return (moved * inverse).astype(BF16)


def picked(goal, first, size):
    return (iota((size, goal.shape[1]), 0) + first == goal).astype(BF16)


def put_pair(ref, at, unit):
    rows = unit.shape[0]
    for c in range(unit.shape[1] // LANES):
        ref[at + c * rows : at + (c + 1) * rows, :] = unit[:, c * LANES : (c + 1) * LANES]


def put_block(ref, unit, meta):
    rows = unit.shape[0] // PLANE
    tall = ref.shape[0] // PLANE - 1
    for p in range(PLANE):
        put_pair(ref, p * tall, unit[p * rows : (p + 1) * rows])
    ref[PLANE * tall :, :] = meta.astype(BF16)


def put_blocks(outs, shifts, goal, meta_ref, emb_ref, per_pair):
    size = PLANE * per_pair
    unit = scaled(dot(picked(goal, 0, size * len(outs)), emb_ref[...]))
    for k, (shift, out_ref) in enumerate(zip(shifts, outs)):
        put_block(out_ref, unit[k * size : (k + 1) * size], meta_ref[shift * PLANE : (shift + 1) * PLANE, :])


def first_kernel(owners, per_owner, per_pair, cid_hbm, idx_hbm, emb_hbm, *refs):
    *outs, pos_ref, meta_ref, flag_ref, emb_ref, cid_ref, idx_ref, sem = refs
    copies = [
        pltpu.make_async_copy(src, dst, sem.at[n])
        for n, (src, dst) in enumerate(((cid_hbm, cid_ref), (idx_hbm, idx_ref)))
    ]
    half = emb_ref.shape[0] // 2
    for n in range(2):
        at = pl.ds(n * half, half)
        copies.append(pltpu.make_async_copy(emb_hbm.at[at], emb_ref.at[at], sem.at[2 + n]))
    for copy in copies:
        copy.start()
    copies[0].wait()
    copies[1].wait()
    pos, meta = route(owners, per_owner, per_pair, wide_row(cid_ref), wide_row(idx_ref))
    put_row(pos_ref, pos)
    meta_ref[...] = meta
    flag_ref[0] = 1
    goal = place(pos, per_pair, SOON, False)
    pick = picked(goal, 0, PLANE * per_pair)
    copies[2].wait()
    moved = dot(pick[:, :half], emb_ref[:half, :])
    copies[3].wait()
    moved = moved + dot(pick[:, half:], emb_ref[half:, :])
    shift = SOON[0]
    put_block(outs[0], scaled(moved), meta[shift * PLANE : (shift + 1) * PLANE])


def some_kernel(per_pair, shifts, pos_ref, meta_ref, emb_ref, *outs):
    goal = place(wide_row(pos_ref), per_pair, shifts, False)
    put_blocks(outs, shifts, goal, meta_ref, emb_ref, per_pair)


def rest_kernel(per_pair, shifts, pos_ref, meta_ref, emb_ref, *refs):
    *outs, late_ref = refs
    some_kernel(per_pair, shifts, pos_ref, meta_ref, emb_ref, *outs)
    goal = place(wide_row(pos_ref), per_pair, LATE, True)
    some = len(LATE) * per_pair
    tall = emb_ref.shape[1] // LANES * per_pair
    step = 4
    for p0 in range(0, PLANE, step):
        unit = scaled(dot(picked(goal, p0 * some, step * some), emb_ref[...]))
        for p in range(p0, p0 + step):
            for k in range(len(LATE)):
                at = ((p - p0) * len(LATE) + k) * per_pair
                put_pair(late_ref.at[p], k * tall, unit[at : at + per_pair])
            meta = [meta_ref[shift * PLANE + p : shift * PLANE + p + 1, :] for shift in LATE]
            meta.append(jnp.zeros((META - len(LATE), LANES), F32))
            late_ref[p, len(LATE) * tall :, :] = jnp.concatenate(meta, axis=0).astype(BF16)


def cut_kernel(got_ref, *outs):
    tall = outs[0].shape[0] // PLANE - 1
    meta = got_ref[:, len(outs) * tall :, :].astype(F32)
    for k, out_ref in enumerate(outs):
        for p in range(PLANE):
            out_ref[p * tall : (p + 1) * tall, :] = got_ref[p, k * tall : (k + 1) * tall, :]
        out_ref[PLANE * tall :, :] = meta[:, k, :].astype(BF16)


def merge_kernel(*refs):
    *ins, out_ref = refs
    tall = ins[0].shape[0] // PLANE - 1
    metas = [ref[PLANE * tall :, :].astype(F32) for ref in ins]
    for p in range(PLANE):
        for k, ref in enumerate(ins):
            out_ref[p, k * tall : (k + 1) * tall, :] = ref[p * tall : (p + 1) * tall, :]
        meta = [m[p : p + 1, :] for m in metas] + [jnp.zeros((META - len(ins), LANES), F32)]
        out_ref[p, len(ins) * tall :, :] = jnp.concatenate(meta, axis=0).astype(BF16)


def piece_weights(lane, per_pair):
    piece = lane // per_pair
    value = jnp.where(piece == 0, 1.0, jnp.where(piece == 1, 256.0, jnp.where(piece == 2, 65536.0, 0.0)))
    return value.astype(BF16)


def best_kernel(per_pair, last, early_hbm, *refs):
    *blocks, out_ref, early_ref, col_scr, group_scr, row_scr, across_scr, sem = refs
    seen_ref = blocks.pop() if last else None
    copy = pltpu.make_async_copy(early_hbm, early_ref, sem)
    copy.start()
    tall = blocks[0].shape[0] // PLANE - 1
    chunks = tall // per_pair
    span = float(1 << INDEX_BITS)
    tiles = col_scr.shape[0] // TILE
    across_scr[...] = jnp.full(across_scr.shape, -1.0, F32)

    def block(t):
        return blocks[t if t < MID.start else t - len(MID)]

    def pairs(t, at):
        if t in MID:
            at += (t - MID.start) * tall
            return early_ref[:, at : at + per_pair, :].reshape(TILE, LANES)
        ref = block(t)
        return jnp.concatenate([ref[p * tall + at : p * tall + at + per_pair, :] for p in range(PLANE)], axis=0)

    def tile(t):
        return jnp.concatenate([pairs(t, c * per_pair) for c in range(chunks)], axis=1)

    def keys(first, metas):
        size = len(metas) * TILE
        at = slice(first * TILE, first * TILE + size)
        meta = jnp.concatenate(metas, axis=0)[:, None, :]
        meta = jnp.broadcast_to(meta, (size // per_pair, per_pair, LANES)).reshape(size, LANES)
        own = (iota((size, LANES), 0) % per_pair) == (iota((size, LANES), 1) % per_pair)
        meta = jnp.where(own, meta, 0.0).astype(BF16)
        col = dot(meta, piece_weights(iota((LANES, LANES), 0), per_pair))
        col_scr[at, :] = col
        group_scr[at, :] = jnp.floor(col * (1.0 / span))
        row_scr[:, at] = dot_t(piece_weights(iota((8, LANES), 1), per_pair), meta)

    best = {}

    def compare(i, j):
        at = slice(j * TILE, (j + 1) * TILE)
        scores = dot_t(tile(j), tile(i))
        col, col_group = col_scr[at, :], group_scr[at, :]
        across = across_scr[at, :]
        for b in range(TILE // LANES):
            n = i * (TILE // LANES) + b
            row = row_scr[0:1, n * LANES : (n + 1) * LANES]
            group = jnp.floor(row * (1.0 / span))
            part = jnp.where(col_group == group, scores[:, b * LANES : (b + 1) * LANES], -1.0)
            before = col < row
            high = jnp.max(jnp.where(before, part, -1.0), axis=0, keepdims=True)
            best[n] = jnp.maximum(best[n], high) if n in best else high
            if j < i:
                across = jnp.maximum(across, jnp.where(before, -1.0, part))
        if j < i:
            across_scr[at, :] = across

    new = range(MID.stop, tiles) if last else range(tiles)
    todo = [(i, j) for i in new for j in range(i + 1)]
    keys(0, [block(t)[PLANE * tall :, :].astype(F32) for t in range(MID.start)])
    if last:
        keys(MID.stop, [block(t)[PLANE * tall :, :].astype(F32) for t in new])
    for i, j in todo:
        if i not in MID and j not in MID:
            compare(i, j)
    copy.wait()
    meta = early_ref[:, len(MID) * tall :, :].astype(F32)
    keys(MID.start, [meta[:, k, :] for k in range(len(MID))])
    for i, j in todo:
        if i in MID or j in MID:
            compare(i, j)

    total = None
    for t in range(tiles):
        parts = []
        for b in range(TILE // LANES):
            n = t * (TILE // LANES) + b
            at = slice(n * LANES, (n + 1) * LANES)
            part = jnp.max(across_scr[at, :].T, axis=0, keepdims=True)
            part = jnp.maximum(part, best[n] if n in best else seen_ref[0:1, at])
            parts.append(part)
            if not last:
                out_ref[0:1, at] = part
        if last:
            place_in = iota((1, TILE), 1)
            plane = place_in // per_pair
            z = (my_z() + NZ - ORDER[t]) % NZ
            home = plane // CORES * (CORES * NZ) + z * CORES + plane % CORES
            to = (iota((out_ref.shape[0], TILE), 0) == home).astype(BF16)
            own = iota((per_pair, TILE), 0) == place_in % per_pair
            rest = jnp.where(own, jnp.concatenate(parts, axis=1), 0.0)
            for _ in range(3):
                piece = rest.astype(BF16)
                rest = rest - piece.astype(F32)
                add = dot_t(to, piece)
                total = add if total is None else total + add
    if last:
        out_ref[...] = total


def home_kernel(ret_ref, pos_ref, out_ref):
    owners, per_pair = ret_ref.shape
    pos = wide_row(pos_ref)
    rows = pos.shape[1]
    owner = pos // per_pair
    rank = pos - owner * per_pair
    slot = (iota((per_pair, rows), 0) == rank).astype(BF16)
    rest = ret_ref[...]
    spread = jnp.zeros((owners, rows), F32)
    for _ in range(3):
        part = rest.astype(BF16)
        rest = rest - part.astype(F32)
        spread = spread + dot(part, slot)
    mine = jnp.where(iota((owners, rows), 0) == owner, spread, 0.0)
    put_row(out_ref, jnp.sum(mine, axis=0, keepdims=True))


def whole(shape):
    return pl.BlockSpec(shape, lambda *_: (0,) * len(shape))


ANY = pl.BlockSpec(memory_space=pl.ANY)
VMEM = pl.BlockSpec(memory_space=pltpu.VMEM)
LIMIT = pltpu.CompilerParams(vmem_limit_bytes=24 * 1024 * 1024)


def in_hbm(*arrays):
    return [pltpu.with_memory_space_constraint(x, pltpu.HBM) for x in arrays]


def shape(dims, dtype):
    return jax.ShapeDtypeStruct(dims, dtype)


def cost(macs):
    return pl.CostEstimate(flops=2 * macs, bytes_accessed=8 << 20, transcendentals=0)


def to_shift(rows, dz):
    members = lax.axis_size("member")
    pairs = []
    for i in range(members):
        z = (i // CORES) % NZ
        pairs.append((i, i + ((z + dz) % NZ - z) * CORES))
    return lax.ppermute(rows, "member", pairs)


def in_plane(rows):
    members = lax.axis_size("member")
    groups = [[i for i in range(members) if (i // CORES) % NZ == z] for z in range(NZ)]
    return lax.all_to_all(rows, "member", split_axis=0, concat_axis=0, tiled=True, axis_index_groups=groups)


def step_of_its_own(run, flag, *args):
    kinds = jax.eval_shape(run, *args)
    skip = lambda *_: jax.tree.map(lambda kind: jnp.zeros(kind.shape, kind.dtype), kinds)
    return lax.cond(flag[0] > 0, run, skip, *args)


def on_device(embeds, cluster_id, row_index):
    members = lax.axis_size("member")
    rows, width = embeds.shape
    per_owner = CLUSTERS // members
    per_pair = rows // members
    lines = rows // LANES
    tall = width // LANES * per_pair
    block = (PLANE * (tall + 1), LANES)
    *parts, pos, meta, flag, kept = pl.pallas_call(
        functools.partial(first_kernel, members, per_owner, per_pair),
        in_specs=[ANY, ANY, ANY],
        out_specs=[whole(block) for _ in SOON]
        + [whole((lines, LANES)), whole((members, LANES)), pl.BlockSpec(memory_space=pltpu.SMEM), VMEM],
        out_shape=[shape(block, BF16) for _ in SOON]
        + [
            shape((lines, LANES), I32),
            shape((members, LANES), F32),
            shape((1,), I32),
            pltpu.VMEM((rows, width), BF16),
        ],
        scratch_shapes=[
            pltpu.VMEM((lines, LANES), I32),
            pltpu.VMEM((lines, LANES), I32),
            pltpu.SemaphoreType.DMA((4,)),
        ],
        compiler_params=LIMIT,
        cost_estimate=cost(TILE * rows * width),
        name="send_first",
    )(*in_hbm(cluster_id.reshape(lines, LANES), row_index.reshape(lines, LANES), embeds))
    got = {dz: to_shift(x, dz) for x, dz in zip(parts, SOON)}

    def send(kernel, shifts, more, name):
        return pl.pallas_call(
            functools.partial(kernel, per_pair, shifts),
            in_specs=[whole((lines, LANES)), whole((members, LANES)), VMEM],
            out_shape=[shape(block, BF16) for _ in shifts] + more,
            compiler_params=LIMIT,
            cost_estimate=cost(len(shifts) * TILE * rows * width),
            name=name,
        )

    *parts, late = send(
        rest_kernel, NEXT, [shape((PLANE, len(LATE) * tall + META, LANES), BF16)], "send_rest"
    )(pos, meta, kept)
    got |= {dz: to_shift(x, dz) for x, dz in zip(parts, NEXT)}

    def late_part(late):
        late = in_plane(late)
        parts = pl.pallas_call(
            cut_kernel, out_shape=[shape(block, BF16) for _ in LATE], compiler_params=LIMIT, name="cut"
        )(late)
        return parts

    moving = step_of_its_own(late_part, flag, late)
    shifted = [to_shift(x, dz) if dz else x for x, dz in zip(moving, LATE)]

    def last_part(got):
        early = pl.pallas_call(
            merge_kernel,
            out_shape=shape((PLANE, len(got) * tall + META, LANES), BF16),
            compiler_params=LIMIT,
            name="merge",
        )(*got)
        return in_plane(early)

    early = step_of_its_own(last_part, flag, [got[dz] for dz in EARLY])
    shifted = dict(zip(LATE, shifted))

    def best_of(last, more, out, tiles, name):
        blocks = [shifted[dz] for n, dz in enumerate(ORDER[:tiles]) if n not in MID] + more
        size = tiles * TILE
        return pl.pallas_call(
            functools.partial(best_kernel, per_pair, last),
            in_specs=[ANY] + [whole(x.shape) for x in blocks],
            out_shape=shape(out, F32),
            scratch_shapes=[
                pltpu.VMEM((PLANE, len(EARLY) * tall + META, LANES), BF16),
                pltpu.VMEM((size, LANES), F32),
                pltpu.VMEM((size, LANES), F32),
                pltpu.VMEM((8, size), F32),
                pltpu.VMEM((size, LANES), F32),
                pltpu.SemaphoreType.DMA,
            ],
            compiler_params=LIMIT,
            cost_estimate=cost(size * size * width // 2),
            name=name,
        )(early, *blocks)

    seen = best_of(False, [], (8, MID.stop * TILE), MID.stop, "best_early")
    best = best_of(True, [seen], (members, per_pair), len(ORDER), "best_last")
    back = lax.all_to_all(best, "member", split_axis=0, concat_axis=0, tiled=True)
    nearest = pl.pallas_call(
        home_kernel,
        out_shape=shape((lines, LANES), F32),
        compiler_params=LIMIT,
        name="home",
    )(back, pos)
    return nearest.reshape(rows)


def solution(mesh):
    in_specs = (P(("outer", "member"), None), P(("outer", "member")), P(("outer", "member")))
    out_specs = P(("outer", "member"))
    return jax.shard_map(
        on_device, mesh=mesh, in_specs=in_specs, out_specs=out_specs, check_vma=False
    )
```

```python
import functools

import jax
import jax.numpy as jnp
from jax import lax
from jax.experimental import pallas as pl
from jax.experimental.pallas import tpu as pltpu
from jax.sharding import PartitionSpec as P

CLUSTERS = 256
INDEX_BITS = 17
LANES = 128
META = 8
TILE = 256
NZ, CORES, PLANE = 8, 2, 8
EARLY = (4, 3, 5)
LATE = (2, 6, 1, 7, 0)
SOON, NEXT = (4,), (3, 5)
ORDER = (2, 6, 0, 4, 3, 5, 1, 7)
MID = range(3, 6)
BF16, F32, I32 = jnp.bfloat16, jnp.float32, jnp.int32


def iota(shape, dim):
    return lax.broadcasted_iota(I32, shape, dim)


def dot(a, b):
    return jnp.dot(a, b, preferred_element_type=F32)


def dot_t(a, b):
    return lax.dot_general(a, b, (((1,), (1,)), ((), ())), preferred_element_type=F32)


def bf16_parts(x):
    parts = []
    for _ in range(3):
        parts.append(x.astype(BF16))
        x = x - parts[-1].astype(F32)
    return parts


def wide_row(ref):
    return jnp.concatenate([ref[b : b + 1, :] for b in range(ref.shape[0])], axis=1)


def put_row(ref, row):
    for b in range(ref.shape[0]):
        ref[b : b + 1, :] = row[:, b * LANES : (b + 1) * LANES]


def my_z():
    return (lax.axis_index("member") // CORES) % NZ


def shift_plane(owner):
    dz = ((owner // CORES) % NZ + NZ - my_z()) % NZ
    return dz, owner // (CORES * NZ) * CORES + owner % CORES


def route(owners, per_owner, per_pair, cid, idx):
    rows = cid.shape[1]
    owner = cid // per_owner
    dz, plane = shift_plane(owner)
    hot = (iota((owners, rows), 0) == dz * PLANE + plane).astype(BF16)
    before = (iota((TILE, TILE), 0) < iota((TILE, TILE), 1)).astype(BF16)
    carry = jnp.zeros((owners, 1), F32)
    ranks = []
    for b in range(rows // TILE):
        part = hot[:, b * TILE : (b + 1) * TILE]
        wide = part.astype(F32)
        ranks.append(jnp.sum((dot(part, before) + carry) * wide, axis=0, keepdims=True))
        carry = carry + jnp.sum(wide, axis=1, keepdims=True)
    rank = jnp.concatenate(ranks, axis=1).astype(I32)
    key = (cid - owner * per_owner) * (1 << INDEX_BITS) + idx
    slot = iota((per_pair, rows), 0) == rank
    pieces = (key & 255, (key >> 8) & 255, key >> 16)
    spread = [jnp.where(slot, p.astype(F32), 0.0).astype(BF16) for p in pieces]
    spread.append(jnp.zeros((LANES - 3 * per_pair, rows), BF16))
    meta = dot_t(hot, jnp.concatenate(spread, axis=0))
    return owner * per_pair + rank, meta


def place(pos, per_pair, shifts, inner):
    owner = pos // per_pair
    rank = pos - owner * per_pair
    dz, plane = shift_plane(owner)
    goal = jnp.full(pos.shape, -1, I32)
    for k, shift in enumerate(shifts):
        slot = plane * len(shifts) + k if inner else k * PLANE + plane
        goal = jnp.where(dz == shift, slot * per_pair + rank, goal)
    return goal


def scaled(moved):
    inverse = lax.rsqrt(jnp.sum(moved * moved, axis=1, keepdims=True) + 1e-06)
    return (moved * inverse).astype(BF16)


def picked(goal, first, size):
    return (iota((size, goal.shape[1]), 0) + first == goal).astype(BF16)


def put_pair(ref, at, unit):
    rows = unit.shape[0]
    for c in range(unit.shape[1] // LANES):
        ref[at + c * rows : at + (c + 1) * rows, :] = unit[:, c * LANES : (c + 1) * LANES]


def put_block(ref, unit, meta):
    rows = unit.shape[0] // PLANE
    tall = ref.shape[0] // PLANE - 1
    for p in range(PLANE):
        put_pair(ref, p * tall, unit[p * rows : (p + 1) * rows])
    ref[PLANE * tall :, :] = meta.astype(BF16)


def put_blocks(outs, shifts, goal, meta_ref, emb_ref, per_pair):
    size = PLANE * per_pair
    unit = scaled(dot(picked(goal, 0, size * len(outs)), emb_ref[...]))
    for k, (shift, out_ref) in enumerate(zip(shifts, outs)):
        put_block(out_ref, unit[k * size : (k + 1) * size], meta_ref[shift * PLANE : (shift + 1) * PLANE, :])


def first_kernel(owners, per_owner, per_pair, cid_hbm, idx_hbm, emb_hbm, *refs):
    *outs, pos_ref, meta_ref, flag_ref, emb_ref, cid_ref, idx_ref, sem = refs
    copies = [
        pltpu.make_async_copy(src, dst, sem.at[n])
        for n, (src, dst) in enumerate(((cid_hbm, cid_ref), (idx_hbm, idx_ref)))
    ]
    half = emb_ref.shape[0] // 2
    for n in range(2):
        at = pl.ds(n * half, half)
        copies.append(pltpu.make_async_copy(emb_hbm.at[at], emb_ref.at[at], sem.at[2 + n]))
    for copy in copies:
        copy.start()
    copies[0].wait()
    copies[1].wait()
    pos, meta = route(owners, per_owner, per_pair, wide_row(cid_ref), wide_row(idx_ref))
    put_row(pos_ref, pos)
    meta_ref[...] = meta
    flag_ref[0] = 1
    goal = place(pos, per_pair, SOON, False)
    pick = picked(goal, 0, PLANE * per_pair)
    copies[2].wait()
    moved = dot(pick[:, :half], emb_ref[:half, :])
    copies[3].wait()
    moved = moved + dot(pick[:, half:], emb_ref[half:, :])
    shift = SOON[0]
    put_block(outs[0], scaled(moved), meta[shift * PLANE : (shift + 1) * PLANE])


def some_kernel(per_pair, shifts, pos_ref, meta_ref, emb_ref, *outs):
    goal = place(wide_row(pos_ref), per_pair, shifts, False)
    put_blocks(outs, shifts, goal, meta_ref, emb_ref, per_pair)


def rest_kernel(per_pair, shifts, pos_ref, meta_ref, emb_ref, *refs):
    *outs, late_ref = refs
    some_kernel(per_pair, shifts, pos_ref, meta_ref, emb_ref, *outs)
    goal = place(wide_row(pos_ref), per_pair, LATE, True)
    some = len(LATE) * per_pair
    tall = emb_ref.shape[1] // LANES * per_pair
    step = 4
    for p0 in range(0, PLANE, step):
        unit = scaled(dot(picked(goal, p0 * some, step * some), emb_ref[...]))
        for p in range(p0, p0 + step):
            for k in range(len(LATE)):
                at = ((p - p0) * len(LATE) + k) * per_pair
                put_pair(late_ref.at[p], k * tall, unit[at : at + per_pair])
            meta = [meta_ref[shift * PLANE + p : shift * PLANE + p + 1, :] for shift in LATE]
            meta.append(jnp.zeros((META - len(LATE), LANES), F32))
            late_ref[p, len(LATE) * tall :, :] = jnp.concatenate(meta, axis=0).astype(BF16)


def cut_kernel(got_ref, *outs):
    tall = outs[0].shape[0] // PLANE - 1
    meta = got_ref[:, len(outs) * tall :, :].astype(F32)
    for k, out_ref in enumerate(outs):
        for p in range(PLANE):
            out_ref[p * tall : (p + 1) * tall, :] = got_ref[p, k * tall : (k + 1) * tall, :]
        out_ref[PLANE * tall :, :] = meta[:, k, :].astype(BF16)


def merge_kernel(*refs):
    *ins, out_ref = refs
    tall = ins[0].shape[0] // PLANE - 1
    metas = [ref[PLANE * tall :, :].astype(F32) for ref in ins]
    for p in range(PLANE):
        for k, ref in enumerate(ins):
            out_ref[p, k * tall : (k + 1) * tall, :] = ref[p * tall : (p + 1) * tall, :]
        meta = [m[p : p + 1, :] for m in metas] + [jnp.zeros((META - len(ins), LANES), F32)]
        out_ref[p, len(ins) * tall :, :] = jnp.concatenate(meta, axis=0).astype(BF16)


def piece_weights(lane, per_pair):
    piece = lane // per_pair
    value = jnp.where(piece == 0, 1.0, jnp.where(piece == 1, 256.0, jnp.where(piece == 2, 65536.0, 0.0)))
    return value.astype(BF16)


def best_kernel(per_pair, last, early_hbm, *refs):
    *blocks, out_ref, early_ref, col_scr, group_scr, row_scr, across_scr, sem = refs
    seen_ref = blocks.pop() if last else None
    copy = pltpu.make_async_copy(early_hbm, early_ref, sem)
    copy.start()
    tall = blocks[0].shape[0] // PLANE - 1
    chunks = tall // per_pair
    span = float(1 << INDEX_BITS)
    tiles = col_scr.shape[0] // TILE
    across_scr[...] = jnp.full(across_scr.shape, -1.0, F32)

    def block(t):
        return blocks[t if t < MID.start else t - len(MID)]

    def pairs(t, at):
        if t in MID:
            at += (t - MID.start) * tall
            return early_ref[:, at : at + per_pair, :].reshape(TILE, LANES)
        ref = block(t)
        return jnp.concatenate([ref[p * tall + at : p * tall + at + per_pair, :] for p in range(PLANE)], axis=0)

    def tile(t):
        return jnp.concatenate([pairs(t, c * per_pair) for c in range(chunks)], axis=1)

    def keys(first, metas):
        size = len(metas) * TILE
        at = slice(first * TILE, first * TILE + size)
        meta = jnp.concatenate(metas, axis=0)[:, None, :]
        meta = jnp.broadcast_to(meta, (size // per_pair, per_pair, LANES)).reshape(size, LANES)
        own = (iota((size, LANES), 0) % per_pair) == (iota((size, LANES), 1) % per_pair)
        meta = jnp.where(own, meta, 0.0).astype(BF16)
        col = dot(meta, piece_weights(iota((LANES, LANES), 0), per_pair))
        col_scr[at, :] = col
        group_scr[at, :] = jnp.floor(col * (1.0 / span))
        row_scr[:, at] = dot_t(piece_weights(iota((8, LANES), 1), per_pair), meta)

    best = {}

    def compare(i, j):
        at = slice(j * TILE, (j + 1) * TILE)
        scores = dot_t(tile(j), tile(i))
        col, col_group = col_scr[at, :], group_scr[at, :]
        across = across_scr[at, :]
        for b in range(TILE // LANES):
            n = i * (TILE // LANES) + b
            row = row_scr[0:1, n * LANES : (n + 1) * LANES]
            group = jnp.floor(row * (1.0 / span))
            part = jnp.where(col_group == group, scores[:, b * LANES : (b + 1) * LANES], -1.0)
            before = col < row
            high = jnp.max(jnp.where(before, part, -1.0), axis=0, keepdims=True)
            best[n] = jnp.maximum(best[n], high) if n in best else high
            if j < i:
                across = jnp.maximum(across, jnp.where(before, -1.0, part))
        if j < i:
            across_scr[at, :] = across

    new = range(MID.stop, tiles) if last else range(tiles)
    todo = [(i, j) for i in new for j in range(i + 1)]
    keys(0, [block(t)[PLANE * tall :, :].astype(F32) for t in range(MID.start)])
    if last:
        keys(MID.stop, [block(t)[PLANE * tall :, :].astype(F32) for t in new])
    for i, j in todo:
        if i not in MID and j not in MID:
            compare(i, j)
    copy.wait()
    meta = early_ref[:, len(MID) * tall :, :].astype(F32)
    keys(MID.start, [meta[:, k, :] for k in range(len(MID))])
    for i, j in todo:
        if i in MID or j in MID:
            compare(i, j)

    total = None
    for t in range(tiles):
        parts = []
        for b in range(TILE // LANES):
            n = t * (TILE // LANES) + b
            at = slice(n * LANES, (n + 1) * LANES)
            part = jnp.max(across_scr[at, :].T, axis=0, keepdims=True)
            part = jnp.maximum(part, best[n] if n in best else seen_ref[0:1, at])
            parts.append(part)
            if not last:
                out_ref[0:1, at] = part
        if last:
            place_in = iota((1, TILE), 1)
            plane = place_in // per_pair
            z = (my_z() + NZ - ORDER[t]) % NZ
            home = plane // CORES * (CORES * NZ) + z * CORES + plane % CORES
            to = (iota((out_ref.shape[0], TILE), 0) == home).astype(BF16)
            own = iota((per_pair, TILE), 0) == place_in % per_pair
            rest = jnp.where(own, jnp.concatenate(parts, axis=1), 0.0)
            add = dot_t(to, jnp.concatenate(bf16_parts(rest), axis=0))
            total = add if total is None else total + add
    if last:
        out_ref[...] = sum(total[:, n * per_pair : (n + 1) * per_pair] for n in range(3))


def home_kernel(ret_ref, pos_ref, out_ref):
    owners, per_pair = ret_ref.shape
    pos = wide_row(pos_ref)
    rows = pos.shape[1]
    owner = pos // per_pair
    rank = pos - owner * per_pair
    slot = (iota((per_pair, rows), 0) == rank).astype(BF16)
    spread = dot(jnp.concatenate(bf16_parts(ret_ref[...]), axis=1), jnp.concatenate([slot] * 3, axis=0))
    mine = jnp.where(iota((owners, rows), 0) == owner, spread, 0.0)
    put_row(out_ref, jnp.sum(mine, axis=0, keepdims=True))


def whole(shape):
    return pl.BlockSpec(shape, lambda *_: (0,) * len(shape))


ANY = pl.BlockSpec(memory_space=pl.ANY)
VMEM = pl.BlockSpec(memory_space=pltpu.VMEM)
LIMIT = pltpu.CompilerParams(vmem_limit_bytes=24 * 1024 * 1024)


def in_hbm(*arrays):
    return [pltpu.with_memory_space_constraint(x, pltpu.HBM) for x in arrays]


def shape(dims, dtype):
    return jax.ShapeDtypeStruct(dims, dtype)


def cost(macs):
    return pl.CostEstimate(flops=2 * macs, bytes_accessed=8 << 20, transcendentals=0)


def to_shift(rows, dz):
    members = lax.axis_size("member")
    pairs = []
    for i in range(members):
        z = (i // CORES) % NZ
        pairs.append((i, i + ((z + dz) % NZ - z) * CORES))
    return lax.ppermute(rows, "member", pairs)


def in_plane(rows):
    members = lax.axis_size("member")
    groups = [[i for i in range(members) if (i // CORES) % NZ == z] for z in range(NZ)]
    return lax.all_to_all(rows, "member", split_axis=0, concat_axis=0, tiled=True, axis_index_groups=groups)


def step_of_its_own(run, flag, *args):
    kinds = jax.eval_shape(run, *args)
    skip = lambda *_: jax.tree.map(lambda kind: jnp.zeros(kind.shape, kind.dtype), kinds)
    return lax.cond(flag[0] > 0, run, skip, *args)


def on_device(embeds, cluster_id, row_index):
    members = lax.axis_size("member")
    rows, width = embeds.shape
    per_owner = CLUSTERS // members
    per_pair = rows // members
    lines = rows // LANES
    tall = width // LANES * per_pair
    block = (PLANE * (tall + 1), LANES)
    *parts, pos, meta, flag, kept = pl.pallas_call(
        functools.partial(first_kernel, members, per_owner, per_pair),
        in_specs=[ANY, ANY, ANY],
        out_specs=[whole(block) for _ in SOON]
        + [whole((lines, LANES)), whole((members, LANES)), pl.BlockSpec(memory_space=pltpu.SMEM), VMEM],
        out_shape=[shape(block, BF16) for _ in SOON]
        + [
            shape((lines, LANES), I32),
            shape((members, LANES), F32),
            shape((1,), I32),
            pltpu.VMEM((rows, width), BF16),
        ],
        scratch_shapes=[
            pltpu.VMEM((lines, LANES), I32),
            pltpu.VMEM((lines, LANES), I32),
            pltpu.SemaphoreType.DMA((4,)),
        ],
        compiler_params=LIMIT,
        cost_estimate=cost(TILE * rows * width),
        name="send_first",
    )(*in_hbm(cluster_id.reshape(lines, LANES), row_index.reshape(lines, LANES), embeds))
    got = {dz: to_shift(x, dz) for x, dz in zip(parts, SOON)}

    def send(kernel, shifts, more, name):
        return pl.pallas_call(
            functools.partial(kernel, per_pair, shifts),
            in_specs=[whole((lines, LANES)), whole((members, LANES)), VMEM],
            out_shape=[shape(block, BF16) for _ in shifts] + more,
            compiler_params=LIMIT,
            cost_estimate=cost(len(shifts) * TILE * rows * width),
            name=name,
        )

    *parts, late = send(
        rest_kernel, NEXT, [shape((PLANE, len(LATE) * tall + META, LANES), BF16)], "send_rest"
    )(pos, meta, kept)
    got |= {dz: to_shift(x, dz) for x, dz in zip(parts, NEXT)}

    def late_part(late):
        late = in_plane(late)
        parts = pl.pallas_call(
            cut_kernel, out_shape=[shape(block, BF16) for _ in LATE], compiler_params=LIMIT, name="cut"
        )(late)
        return parts

    moving = step_of_its_own(late_part, flag, late)
    shifted = [to_shift(x, dz) if dz else x for x, dz in zip(moving, LATE)]

    def last_part(got):
        early = pl.pallas_call(
            merge_kernel,
            out_shape=shape((PLANE, len(got) * tall + META, LANES), BF16),
            compiler_params=LIMIT,
            name="merge",
        )(*got)
        return in_plane(early)

    early = step_of_its_own(last_part, flag, [got[dz] for dz in EARLY])
    shifted = dict(zip(LATE, shifted))

    def best_of(last, more, out, tiles, name):
        blocks = [shifted[dz] for n, dz in enumerate(ORDER[:tiles]) if n not in MID] + more
        size = tiles * TILE
        return pl.pallas_call(
            functools.partial(best_kernel, per_pair, last),
            in_specs=[ANY] + [whole(x.shape) for x in blocks],
            out_shape=shape(out, F32),
            scratch_shapes=[
                pltpu.VMEM((PLANE, len(EARLY) * tall + META, LANES), BF16),
                pltpu.VMEM((size, LANES), F32),
                pltpu.VMEM((size, LANES), F32),
                pltpu.VMEM((8, size), F32),
                pltpu.VMEM((size, LANES), F32),
                pltpu.SemaphoreType.DMA,
            ],
            compiler_params=LIMIT,
            cost_estimate=cost(size * size * width // 2),
            name=name,
        )(early, *blocks)

    seen = best_of(False, [], (8, MID.stop * TILE), MID.stop, "best_early")
    best = best_of(True, [seen], (members, per_pair), len(ORDER), "best_last")
    back = lax.all_to_all(best, "member", split_axis=0, concat_axis=0, tiled=True)
    nearest = pl.pallas_call(
        home_kernel,
        out_shape=shape((lines, LANES), F32),
        compiler_params=LIMIT,
        name="home",
    )(back, pos)
    return nearest.reshape(rows)


def solution(mesh):
    in_specs = (P(("outer", "member"), None), P(("outer", "member")), P(("outer", "member")))
    out_specs = P(("outer", "member"))
    return jax.shard_map(
        on_device, mesh=mesh, in_specs=in_specs, out_specs=out_specs, check_vma=False
    )
```

```python
import functools

import jax
import jax.numpy as jnp
from jax import lax
from jax.experimental import pallas as pl
from jax.experimental.pallas import tpu as pltpu
from jax.sharding import PartitionSpec as P

CLUSTERS = 256
INDEX_BITS = 17
LANES = 128
META = 8
TILE = 256
NZ, CORES, PLANE = 8, 2, 8
EARLY = (4, 3, 5)
LATE = (2, 6, 1, 7, 0)
SOON, NEXT = (4,), (3, 5)
ORDER = (2, 6, 0, 4, 3, 5, 1, 7)
MID = range(3, 6)
BF16, F32, I32 = jnp.bfloat16, jnp.float32, jnp.int32


def iota(shape, dim):
    return lax.broadcasted_iota(I32, shape, dim)


def dot(a, b):
    return jnp.dot(a, b, preferred_element_type=F32)


def dot_t(a, b):
    return lax.dot_general(a, b, (((1,), (1,)), ((), ())), preferred_element_type=F32)


def wide_row(ref):
    return jnp.concatenate([ref[b : b + 1, :] for b in range(ref.shape[0])], axis=1)


def put_row(ref, row):
    for b in range(ref.shape[0]):
        ref[b : b + 1, :] = row[:, b * LANES : (b + 1) * LANES]


def my_z():
    return (lax.axis_index("member") // CORES) % NZ


def shift_plane(owner):
    dz = ((owner // CORES) % NZ + NZ - my_z()) % NZ
    return dz, owner // (CORES * NZ) * CORES + owner % CORES


def route(owners, per_owner, per_pair, cid, idx):
    rows = cid.shape[1]
    owner = cid // per_owner
    dz, plane = shift_plane(owner)
    hot = (iota((owners, rows), 0) == dz * PLANE + plane).astype(BF16)
    before = (iota((TILE, TILE), 0) < iota((TILE, TILE), 1)).astype(BF16)
    carry = jnp.zeros((owners, 1), F32)
    ranks = []
    for b in range(rows // TILE):
        part = hot[:, b * TILE : (b + 1) * TILE]
        wide = part.astype(F32)
        ranks.append(jnp.sum((dot(part, before) + carry) * wide, axis=0, keepdims=True))
        carry = carry + jnp.sum(wide, axis=1, keepdims=True)
    rank = jnp.concatenate(ranks, axis=1).astype(I32)
    key = (cid - owner * per_owner) * (1 << INDEX_BITS) + idx
    slot = iota((per_pair, rows), 0) == rank
    pieces = (key & 255, (key >> 8) & 255, key >> 16)
    spread = [jnp.where(slot, p.astype(F32), 0.0).astype(BF16) for p in pieces]
    spread.append(jnp.zeros((LANES - 3 * per_pair, rows), BF16))
    meta = dot_t(hot, jnp.concatenate(spread, axis=0))
    return owner * per_pair + rank, meta


def place(pos, per_pair, shifts, inner):
    owner = pos // per_pair
    rank = pos - owner * per_pair
    dz, plane = shift_plane(owner)
    goal = jnp.full(pos.shape, -1, I32)
    for k, shift in enumerate(shifts):
        slot = plane * len(shifts) + k if inner else k * PLANE + plane
        goal = jnp.where(dz == shift, slot * per_pair + rank, goal)
    return goal


def scaled(moved):
    inverse = lax.rsqrt(jnp.sum(moved * moved, axis=1, keepdims=True) + 1e-06)
    return (moved * inverse).astype(BF16)


def picked(goal, first, size):
    return (iota((size, goal.shape[1]), 0) + first == goal).astype(BF16)


def put_pair(ref, at, unit):
    rows = unit.shape[0]
    for c in range(unit.shape[1] // LANES):
        ref[at + c * rows : at + (c + 1) * rows, :] = unit[:, c * LANES : (c + 1) * LANES]


def put_block(ref, unit, meta):
    rows = unit.shape[0] // PLANE
    tall = ref.shape[0] // PLANE - 1
    for p in range(PLANE):
        put_pair(ref, p * tall, unit[p * rows : (p + 1) * rows])
    ref[PLANE * tall :, :] = meta.astype(BF16)


def put_blocks(outs, shifts, goal, meta_ref, emb_ref, per_pair):
    size = PLANE * per_pair
    unit = scaled(dot(picked(goal, 0, size * len(outs)), emb_ref[...]))
    for k, (shift, out_ref) in enumerate(zip(shifts, outs)):
        put_block(out_ref, unit[k * size : (k + 1) * size], meta_ref[shift * PLANE : (shift + 1) * PLANE, :])


def first_kernel(owners, per_owner, per_pair, cid_hbm, idx_hbm, emb_hbm, *refs):
    *outs, pos_ref, meta_ref, flag_ref, emb_ref, cid_ref, idx_ref, sem = refs
    copies = [
        pltpu.make_async_copy(src, dst, sem.at[n])
        for n, (src, dst) in enumerate(((cid_hbm, cid_ref), (idx_hbm, idx_ref)))
    ]
    half = emb_ref.shape[0] // 2
    for n in range(2):
        at = pl.ds(n * half, half)
        copies.append(pltpu.make_async_copy(emb_hbm.at[at], emb_ref.at[at], sem.at[2 + n]))
    for copy in copies:
        copy.start()
    copies[0].wait()
    copies[1].wait()
    pos, meta = route(owners, per_owner, per_pair, wide_row(cid_ref), wide_row(idx_ref))
    put_row(pos_ref, pos)
    meta_ref[...] = meta
    flag_ref[0] = 1
    goal = place(pos, per_pair, SOON, False)
    pick = picked(goal, 0, PLANE * per_pair)
    copies[2].wait()
    moved = dot(pick[:, :half], emb_ref[:half, :])
    copies[3].wait()
    moved = moved + dot(pick[:, half:], emb_ref[half:, :])
    shift = SOON[0]
    put_block(outs[0], scaled(moved), meta[shift * PLANE : (shift + 1) * PLANE])


def some_kernel(per_pair, shifts, pos_ref, meta_ref, emb_ref, *outs):
    goal = place(wide_row(pos_ref), per_pair, shifts, False)
    put_blocks(outs, shifts, goal, meta_ref, emb_ref, per_pair)


def rest_kernel(per_pair, shifts, pos_ref, meta_ref, emb_ref, *refs):
    *outs, late_ref = refs
    some_kernel(per_pair, shifts, pos_ref, meta_ref, emb_ref, *outs)
    goal = place(wide_row(pos_ref), per_pair, LATE, True)
    some = len(LATE) * per_pair
    tall = emb_ref.shape[1] // LANES * per_pair
    step = 8
    for p0 in range(0, PLANE, step):
        unit = scaled(dot(picked(goal, p0 * some, step * some), emb_ref[...]))
        for p in range(p0, p0 + step):
            for k in range(len(LATE)):
                at = ((p - p0) * len(LATE) + k) * per_pair
                put_pair(late_ref.at[p], k * tall, unit[at : at + per_pair])
            meta = [meta_ref[shift * PLANE + p : shift * PLANE + p + 1, :] for shift in LATE]
            meta.append(jnp.zeros((META - len(LATE), LANES), F32))
            late_ref[p, len(LATE) * tall :, :] = jnp.concatenate(meta, axis=0).astype(BF16)


def cut_kernel(got_ref, *outs):
    tall = outs[0].shape[0] // PLANE - 1
    meta = got_ref[:, len(outs) * tall :, :].astype(F32)
    for k, out_ref in enumerate(outs):
        for p in range(PLANE):
            out_ref[p * tall : (p + 1) * tall, :] = got_ref[p, k * tall : (k + 1) * tall, :]
        out_ref[PLANE * tall :, :] = meta[:, k, :].astype(BF16)


def merge_kernel(*refs):
    *ins, out_ref = refs
    tall = ins[0].shape[0] // PLANE - 1
    metas = [ref[PLANE * tall :, :].astype(F32) for ref in ins]
    for p in range(PLANE):
        for k, ref in enumerate(ins):
            out_ref[p, k * tall : (k + 1) * tall, :] = ref[p * tall : (p + 1) * tall, :]
        meta = [m[p : p + 1, :] for m in metas] + [jnp.zeros((META - len(ins), LANES), F32)]
        out_ref[p, len(ins) * tall :, :] = jnp.concatenate(meta, axis=0).astype(BF16)


def piece_weights(lane, per_pair):
    piece = lane // per_pair
    value = jnp.where(piece == 0, 1.0, jnp.where(piece == 1, 256.0, jnp.where(piece == 2, 65536.0, 0.0)))
    return value.astype(BF16)


def best_kernel(per_pair, last, early_hbm, *refs):
    *blocks, out_ref, early_ref, col_scr, group_scr, row_scr, across_scr, sem = refs
    seen_ref = blocks.pop() if last else None
    copy = pltpu.make_async_copy(early_hbm, early_ref, sem)
    copy.start()
    tall = blocks[0].shape[0] // PLANE - 1
    chunks = tall // per_pair
    span = float(1 << INDEX_BITS)
    tiles = col_scr.shape[0] // TILE
    across_scr[...] = jnp.full(across_scr.shape, -1.0, F32)

    def block(t):
        return blocks[t if t < MID.start else t - len(MID)]

    def pairs(t, at):
        if t in MID:
            at += (t - MID.start) * tall
            return early_ref[:, at : at + per_pair, :].reshape(TILE, LANES)
        ref = block(t)
        return jnp.concatenate([ref[p * tall + at : p * tall + at + per_pair, :] for p in range(PLANE)], axis=0)

    def tile(t):
        return jnp.concatenate([pairs(t, c * per_pair) for c in range(chunks)], axis=1)

    def keys(first, metas):
        size = len(metas) * TILE
        at = slice(first * TILE, first * TILE + size)
        meta = jnp.concatenate(metas, axis=0)[:, None, :]
        meta = jnp.broadcast_to(meta, (size // per_pair, per_pair, LANES)).reshape(size, LANES)
        own = (iota((size, LANES), 0) % per_pair) == (iota((size, LANES), 1) % per_pair)
        meta = jnp.where(own, meta, 0.0).astype(BF16)
        col = dot(meta, piece_weights(iota((LANES, LANES), 0), per_pair))
        col_scr[at, :] = col
        group_scr[at, :] = jnp.floor(col * (1.0 / span))
        row_scr[:, at] = dot_t(piece_weights(iota((8, LANES), 1), per_pair), meta)

    best = {}

    def compare(i, j):
        at = slice(j * TILE, (j + 1) * TILE)
        scores = dot_t(tile(j), tile(i))
        col, col_group = col_scr[at, :], group_scr[at, :]
        across = across_scr[at, :]
        for b in range(TILE // LANES):
            n = i * (TILE // LANES) + b
            row = row_scr[0:1, n * LANES : (n + 1) * LANES]
            group = jnp.floor(row * (1.0 / span))
            part = jnp.where(col_group == group, scores[:, b * LANES : (b + 1) * LANES], -1.0)
            before = col < row
            high = jnp.max(jnp.where(before, part, -1.0), axis=0, keepdims=True)
            best[n] = jnp.maximum(best[n], high) if n in best else high
            if j < i:
                across = jnp.maximum(across, jnp.where(before, -1.0, part))
        if j < i:
            across_scr[at, :] = across

    new = range(MID.stop, tiles) if last else range(tiles)
    todo = [(i, j) for i in new for j in range(i + 1)]
    keys(0, [block(t)[PLANE * tall :, :].astype(F32) for t in range(MID.start)])
    if last:
        keys(MID.stop, [block(t)[PLANE * tall :, :].astype(F32) for t in new])
    for i, j in todo:
        if i not in MID and j not in MID:
            compare(i, j)
    copy.wait()
    meta = early_ref[:, len(MID) * tall :, :].astype(F32)
    keys(MID.start, [meta[:, k, :] for k in range(len(MID))])
    for i, j in todo:
        if i in MID or j in MID:
            compare(i, j)

    total = None
    for t in range(tiles):
        parts = []
        for b in range(TILE // LANES):
            n = t * (TILE // LANES) + b
            at = slice(n * LANES, (n + 1) * LANES)
            part = jnp.max(across_scr[at, :].T, axis=0, keepdims=True)
            part = jnp.maximum(part, best[n] if n in best else seen_ref[0:1, at])
            parts.append(part)
            if not last:
                out_ref[0:1, at] = part
        if last:
            place_in = iota((1, TILE), 1)
            plane = place_in // per_pair
            z = (my_z() + NZ - ORDER[t]) % NZ
            home = plane // CORES * (CORES * NZ) + z * CORES + plane % CORES
            to = (iota((out_ref.shape[0], TILE), 0) == home).astype(BF16)
            own = iota((per_pair, TILE), 0) == place_in % per_pair
            rest = jnp.where(own, jnp.concatenate(parts, axis=1), 0.0)
            for _ in range(3):
                piece = rest.astype(BF16)
                rest = rest - piece.astype(F32)
                add = dot_t(to, piece)
                total = add if total is None else total + add
    if last:
        out_ref[...] = total


def home_kernel(ret_ref, pos_ref, out_ref):
    owners, per_pair = ret_ref.shape
    pos = wide_row(pos_ref)
    rows = pos.shape[1]
    owner = pos // per_pair
    rank = pos - owner * per_pair
    slot = (iota((per_pair, rows), 0) == rank).astype(BF16)
    rest = ret_ref[...]
    spread = jnp.zeros((owners, rows), F32)
    for _ in range(3):
        part = rest.astype(BF16)
        rest = rest - part.astype(F32)
        spread = spread + dot(part, slot)
    mine = jnp.where(iota((owners, rows), 0) == owner, spread, 0.0)
    put_row(out_ref, jnp.sum(mine, axis=0, keepdims=True))


def whole(shape):
    return pl.BlockSpec(shape, lambda *_: (0,) * len(shape))


ANY = pl.BlockSpec(memory_space=pl.ANY)
VMEM = pl.BlockSpec(memory_space=pltpu.VMEM)
LIMIT = pltpu.CompilerParams(vmem_limit_bytes=24 * 1024 * 1024)


def in_hbm(*arrays):
    return [pltpu.with_memory_space_constraint(x, pltpu.HBM) for x in arrays]


def shape(dims, dtype):
    return jax.ShapeDtypeStruct(dims, dtype)


def cost(macs):
    return pl.CostEstimate(flops=2 * macs, bytes_accessed=8 << 20, transcendentals=0)


def to_shift(rows, dz):
    members = lax.axis_size("member")
    pairs = []
    for i in range(members):
        z = (i // CORES) % NZ
        pairs.append((i, i + ((z + dz) % NZ - z) * CORES))
    return lax.ppermute(rows, "member", pairs)


def in_plane(rows):
    members = lax.axis_size("member")
    groups = [[i for i in range(members) if (i // CORES) % NZ == z] for z in range(NZ)]
    return lax.all_to_all(rows, "member", split_axis=0, concat_axis=0, tiled=True, axis_index_groups=groups)


def step_of_its_own(run, flag, *args):
    kinds = jax.eval_shape(run, *args)
    skip = lambda *_: jax.tree.map(lambda kind: jnp.zeros(kind.shape, kind.dtype), kinds)
    return lax.cond(flag[0] > 0, run, skip, *args)


def on_device(embeds, cluster_id, row_index):
    members = lax.axis_size("member")
    rows, width = embeds.shape
    per_owner = CLUSTERS // members
    per_pair = rows // members
    lines = rows // LANES
    tall = width // LANES * per_pair
    block = (PLANE * (tall + 1), LANES)
    *parts, pos, meta, flag, kept = pl.pallas_call(
        functools.partial(first_kernel, members, per_owner, per_pair),
        in_specs=[ANY, ANY, ANY],
        out_specs=[whole(block) for _ in SOON]
        + [whole((lines, LANES)), whole((members, LANES)), pl.BlockSpec(memory_space=pltpu.SMEM), VMEM],
        out_shape=[shape(block, BF16) for _ in SOON]
        + [
            shape((lines, LANES), I32),
            shape((members, LANES), F32),
            shape((1,), I32),
            pltpu.VMEM((rows, width), BF16),
        ],
        scratch_shapes=[
            pltpu.VMEM((lines, LANES), I32),
            pltpu.VMEM((lines, LANES), I32),
            pltpu.SemaphoreType.DMA((4,)),
        ],
        compiler_params=LIMIT,
        cost_estimate=cost(TILE * rows * width),
        name="send_first",
    )(*in_hbm(cluster_id.reshape(lines, LANES), row_index.reshape(lines, LANES), embeds))
    got = {dz: to_shift(x, dz) for x, dz in zip(parts, SOON)}

    def send(kernel, shifts, more, name):
        return pl.pallas_call(
            functools.partial(kernel, per_pair, shifts),
            in_specs=[whole((lines, LANES)), whole((members, LANES)), VMEM],
            out_shape=[shape(block, BF16) for _ in shifts] + more,
            compiler_params=LIMIT,
            cost_estimate=cost(len(shifts) * TILE * rows * width),
            name=name,
        )

    *parts, late = send(
        rest_kernel, NEXT, [shape((PLANE, len(LATE) * tall + META, LANES), BF16)], "send_rest"
    )(pos, meta, kept)
    got |= {dz: to_shift(x, dz) for x, dz in zip(parts, NEXT)}

    def late_part(late):
        late = in_plane(late)
        parts = pl.pallas_call(
            cut_kernel, out_shape=[shape(block, BF16) for _ in LATE], compiler_params=LIMIT, name="cut"
        )(late)
        return parts

    moving = step_of_its_own(late_part, flag, late)
    shifted = [to_shift(x, dz) if dz else x for x, dz in zip(moving, LATE)]

    def last_part(got):
        early = pl.pallas_call(
            merge_kernel,
            out_shape=shape((PLANE, len(got) * tall + META, LANES), BF16),
            compiler_params=LIMIT,
            name="merge",
        )(*got)
        return in_plane(early)

    early = step_of_its_own(last_part, flag, [got[dz] for dz in EARLY])
    shifted = dict(zip(LATE, shifted))

    def best_of(last, more, out, tiles, name):
        blocks = [shifted[dz] for n, dz in enumerate(ORDER[:tiles]) if n not in MID] + more
        size = tiles * TILE
        return pl.pallas_call(
            functools.partial(best_kernel, per_pair, last),
            in_specs=[ANY] + [whole(x.shape) for x in blocks],
            out_shape=shape(out, F32),
            scratch_shapes=[
                pltpu.VMEM((PLANE, len(EARLY) * tall + META, LANES), BF16),
                pltpu.VMEM((size, LANES), F32),
                pltpu.VMEM((size, LANES), F32),
                pltpu.VMEM((8, size), F32),
                pltpu.VMEM((size, LANES), F32),
                pltpu.SemaphoreType.DMA,
            ],
            compiler_params=LIMIT,
            cost_estimate=cost(size * size * width // 2),
            name=name,
        )(early, *blocks)

    seen = best_of(False, [], (8, MID.stop * TILE), MID.stop, "best_early")
    best = best_of(True, [seen], (members, per_pair), len(ORDER), "best_last")
    back = lax.all_to_all(best, "member", split_axis=0, concat_axis=0, tiled=True)
    nearest = pl.pallas_call(
        home_kernel,
        out_shape=shape((lines, LANES), F32),
        compiler_params=LIMIT,
        name="home",
    )(back, pos)
    return nearest.reshape(rows)


def solution(mesh):
    in_specs = (P(("outer", "member"), None), P(("outer", "member")), P(("outer", "member")))
    out_specs = P(("outer", "member"))
    return jax.shard_map(
        on_device, mesh=mesh, in_specs=in_specs, out_specs=out_specs, check_vma=False
    )
```
